256 devices in a mesh: samp: 64 (over x_hi, y, z), par: 4 (over x_lo, core).
Axes of the slice: x: 4 (x_hi: 2, x_lo: 2; x = x_hi * 2 + x_lo), y: 4, z: 8, core: 2. Of those that a mesh axis runs over, the one named last changes fastest.
Arguments:
- spin_bits: int32 [1024, 100], P('samp'), may hold values from 0 to 1
- flip_energy: float32 [1024], P('samp'), may hold values from -8 to 8
- jacobian: bfloat16 [1024, 786432], P('samp', 'par')
Outputs:
- update: float32 [4, 64, 3072], P('par', 'samp')
The draws below stay inside these ranges and needn't reach their ends.
All inputs are finite; a program needn't handle non-finite values.
Results may differ from the reference program's by a relative error of at most 0.002.
The reference program's roundings to bfloat16 on the way count: a program that leaves them out, or rounds other values in their place, can miss the bound.
Values may be sent and summed in bfloat16 or wider, within the bound.
A program may use at most 128 MiB of HBM per device.

```python
import math
import jax
import jax.numpy as jnp
from jax import lax

SITES = 100
PAR_DEV = 196608
SAMPLES = 1024
PARAMS = 786432
N_SAMP = 64
N_PAR = 4


def draw_jacobian(key, part):
    key = jax.random.fold_in(key, 7)
    subkeys = jax.random.split(key, 5)
    column_ramp = 3.0 ** (0.5 * jnp.arange(PARAMS, dtype=jnp.float32) / PARAMS)
    col_scale = jnp.exp(jax.random.uniform(subkeys[1], (1, PARAMS), jnp.float32, math.log(0.3), math.log(3.0))) * column_ramp[None, :]
    row_scale = jnp.exp(jax.random.uniform(subkeys[0], (SAMPLES, 1), jnp.float32, 0.0, math.log(10.0)))
    fresh_noise = jnp.clip(jax.random.normal(subkeys[2], (SAMPLES, PARAMS), jnp.float32), -6.0, 6.0)
    shared = jnp.clip(jax.random.normal(subkeys[3], (SAMPLES, 1), jnp.float32), -4.0, 4.0)
    loadings = jnp.clip(jax.random.normal(subkeys[4], (1, PARAMS), jnp.float32), -4.0, 4.0)
    common = 0.6 * shared * loadings
    values = row_scale * col_scale * (fresh_noise + common) / math.sqrt(PARAMS)
    return values.astype(jnp.bfloat16)


def set_ends(values, own_key, least, top_value):
    index_at = [jax.random.randint(jax.random.fold_in(own_key, axis), (), 0, length) for axis, length in enumerate(values.shape)]
    longest = values.shape.index(max(values.shape))
    next_to = index_at[:longest] + [(index_at[longest] + 1) % values.shape[longest]] + index_at[longest + 1:]
    return values.at[tuple(index_at)].set(least).at[tuple(next_to)].set(top_value)


def block_levels(key, extent, pieces, least, largest):
    loudness = 1.0
    for dim, shards_of in pieces:
        heights = jax.random.uniform(jax.random.fold_in(jax.random.fold_in(key, 6), dim), (shards_of,), jnp.float32, least / len(pieces), largest / len(pieces))
        loudness = loudness * jnp.repeat(jnp.exp(heights), extent[dim] // shards_of).reshape((-1,) + (1,) * (len(extent) - 1 - dim))
    return loudness


def scatter_about(key, extent, scale, reach, shards=(), held_as=jnp.bfloat16):
    gain = block_levels(key, extent, shards, -0.22, 0.18) if shards else 1.0
    values = jax.random.normal(key, extent, jnp.float32) * scale * gain
    return jnp.minimum(jnp.maximum(values, -reach), reach).astype(held_as)


def setup_inputs(seed: int = 0) -> dict:
    arg_keys = jax.random.split(jax.random.key(seed), 4)
    return {
        "spin_bits": set_ends(jax.random.randint(arg_keys[0], (SAMPLES, SITES), 0, 2), jax.random.fold_in(arg_keys[0], 1), 0, 1).astype(jnp.int32),
        "flip_energy": scatter_about(arg_keys[1], (SAMPLES,), 2.0, 8.0, ((0, 64),), jnp.float32),
        "jacobian": draw_jacobian(jax.random.fold_in(arg_keys[3], 71), 0),
    }


diag_shift = 0.5
coupling_one = 1.0
coupling_two = 0.5

def diagonal_energy(spin_bits):
    lattice_side = math.isqrt(SITES)
    spin_signs = (2 * spin_bits - 1).astype(jnp.float32).reshape(-1, lattice_side, lattice_side)
    east_spins = jnp.roll(spin_signs, -1, axis=2)
    south_spins = jnp.roll(spin_signs, -1, axis=1)
    nearest = lax.optimization_barrier(jnp.sum(spin_signs * east_spins + spin_signs * south_spins, axis=(1, 2)))
    diagonal_one = jnp.roll(south_spins, -1, axis=2)
    diagonal_two = jnp.roll(south_spins, 1, axis=2)
    further = lax.optimization_barrier(jnp.sum(spin_signs * diagonal_one + spin_signs * diagonal_two, axis=(1, 2)))
    return 0.25 * coupling_one * nearest + 0.25 * coupling_two * further

def solve_both(factor, right_side):
    middle = lax.linalg.triangular_solve(factor, right_side[:, None], left_side=True, lower=True)
    result = lax.linalg.triangular_solve(factor, middle, left_side=True, lower=True, transpose_a=True)
    return result[:, 0]

def reference(spin_bits, flip_energy, jacobian):
    energy = diagonal_energy(spin_bits) + flip_energy
    centred_energy = energy - jnp.mean(energy)
    block_width = PAR_DEV // N_SAMP
    block_count = PARAMS // block_width

    def centre(block_index):
        start = (block_index * block_width).astype(jnp.int32)
        column_block = lax.dynamic_slice_in_dim(jacobian, start, block_width, 1).astype(jnp.float32)
        column_mean = lax.optimization_barrier(jnp.mean(column_block, axis=0, keepdims=True))
        return (column_block - column_mean).astype(jnp.bfloat16)

    def accumulate(running, block_index):
        column_block = centre(block_index).astype(jnp.float32)
        product = jnp.dot(column_block, column_block.T, precision=lax.Precision.HIGHEST)
        return (running + product, None)
    gram_total, unused = lax.scan(accumulate, jnp.zeros((SAMPLES, SAMPLES), jnp.float32), jnp.arange(block_count, dtype=jnp.int32))
    shifted = gram_total + diag_shift * jnp.eye(SAMPLES, dtype=jnp.float32)
    factor = jnp.linalg.cholesky(shifted)
    weights = solve_both(factor, centred_energy).astype(jnp.bfloat16)
    wide_weights = weights.astype(jnp.float32)

    def project(block_index):
        column_block = centre(block_index).astype(jnp.float32)
        return jnp.dot(wide_weights, column_block, precision=lax.Precision.HIGHEST)
    direction = lax.map(project, jnp.arange(block_count, dtype=jnp.int32))
    root_mean = jnp.sqrt(jnp.sum(direction * direction) / PARAMS + 1e-06)
    update = -direction / root_mean
    return update.reshape(N_PAR, N_SAMP, block_width)
```

```python
import math

import jax, jax.numpy as jnp
from jax import lax
from jax.experimental import pallas as pl
from jax.experimental.pallas import tpu as pltpu
from jax.sharding import PartitionSpec as P

N = 1024
NB = 128
GR = 8


def split3(x):
    high = x.astype(jnp.bfloat16)
    rest = x - high.astype(jnp.float32)
    mid = rest.astype(jnp.bfloat16)
    low = (rest - mid.astype(jnp.float32)).astype(jnp.bfloat16)
    return high, mid, low


def dot_wide(a, b):
    ah, am, al = split3(a)
    bh, bm, bl = split3(b)
    left = jnp.concatenate([ah, ah, am, am, ah, al], axis=1)
    right = jnp.concatenate([bh, bm, bh, bm, bl, bh], axis=0)
    return jnp.dot(left, right, preferred_element_type=jnp.float32)


def lanes(v, c):
    return jnp.broadcast_to(v[:, c:c + 1], (GR, NB))


def subs(v, r):
    return jnp.broadcast_to(v[r:r + 1, :], (GR, NB))


def invert_block(rows):
    lane = lax.broadcasted_iota(jnp.int32, (GR, NB), 1)
    sub = lax.broadcasted_iota(jnp.int32, (GR, NB), 0)
    count = NB // GR
    for g in range(count):
        base = g * GR
        own = rows[g]
        piv_cols = [lanes(own, base + c) for c in range(GR)]
        in_piv = (lane >= base) & (lane < base + GR)
        row = jnp.where(in_piv, jnp.where(lane - base == sub, 1.0, 0.0), own)
        for q in range(GR):
            at = sub == q
            inv = 1.0 / subs(piv_cols[q], q)
            coef = jnp.where(at, -inv, piv_cols[q] * inv)
            row = jnp.where(at, 0.0, row) - coef * subs(row, q)
            for c in range(q + 1, GR):
                piv_cols[c] = jnp.where(at, 0.0, piv_cols[c]) - coef * subs(piv_cols[c], q)
        spread = [subs(row, q) for q in range(GR)]
        new_rows = []
        for v in range(count):
            if v == g:
                new_rows.append(row)
                continue
            terms = [lanes(rows[v], base + q) * spread[q] for q in range(GR)]
            total = (((terms[0] + terms[1]) + (terms[2] + terms[3]))
                     + ((terms[4] + terms[5]) + (terms[6] + terms[7])))
            new_rows.append(jnp.where(in_piv, 0.0, rows[v]) - total)
        rows = new_rows
    return rows


def solve_kernel(gram_ref, energy_ref, centred_ref, out_ref, work, held, x_row, x_col, sem):
    fetch = pltpu.make_async_copy(centred_ref, held, sem)
    fetch.start()
    sub = lax.broadcasted_iota(jnp.int32, (NB, NB), 0)
    lane = lax.broadcasted_iota(jnp.int32, (NB, NB), 1)
    eye = jnp.where(sub == lane, 1.0, 0.0)
    work[0:N, :] = gram_ref[...]
    for b in range(N // NB):
        at = pl.ds(b * NB, NB)
        work[at, at] = gram_ref[at, at] + 0.5 * eye
    energy = energy_ref[...]
    mean = jnp.sum(energy, axis=1, keepdims=True) * (1.0 / N)
    work[N:N + GR, :] = jnp.broadcast_to(energy - mean, (GR, N))

    def stage(k, carry):
        at = pl.ds(pl.multiple_of(k * NB, NB), NB)
        rows = [work[pl.ds(pl.multiple_of(k * NB + v * GR, GR), GR), at] for v in range(NB // GR)]
        rows = invert_block(rows)
        for v in range(NB // GR):
            work[pl.ds(pl.multiple_of(k * NB + v * GR, GR), GR), at] = rows[v]
        for c in range(N // NB - 1):
            @pl.when(k == c)
            def _():
                own = slice(c * NB, (c + 1) * NB)
                after = slice((c + 1) * NB, N)
                below = slice((c + 1) * NB, N + GR)
                inverse = work[own, own]
                turned = dot_wide(inverse, work[own, after])
                work[below, after] = work[below, after] - dot_wide(work[below, own], turned)
                work[own, after] = turned
        return carry

    lax.fori_loop(0, N // NB, stage, 0)

    for k in range(N // NB - 1, -1, -1):
        own = slice(k * NB, (k + 1) * NB)
        total = work[own, own] * work[N:N + 1, own]
        for j in range(k + 1, N // NB):
            col = slice(j * NB, (j + 1) * NB)
            total = total - work[own, col] * x_row[0:1, col]
        column = jnp.sum(total, axis=1, keepdims=True)
        column = jnp.broadcast_to(column, (NB, NB))
        x_row[0:1, own] = jnp.sum(column * eye, axis=0, keepdims=True)
        x_col[own, :] = column.astype(jnp.bfloat16).astype(jnp.float32)

    weights = x_row[0:1, :].astype(jnp.bfloat16)
    wide = weights.astype(jnp.float32)

    def quad(i, acc):
        at = pl.ds(pl.multiple_of(i * NB, NB), NB)
        part = gram_ref[at, 0:NB] * wide[:, 0:NB]
        for j in range(1, N // NB):
            col = slice(j * NB, (j + 1) * NB)
            part = part + gram_ref[at, col] * wide[:, col]
        return acc + part * x_col[at, :]

    acc = lax.fori_loop(0, N // NB, quad, jnp.zeros((NB, NB), jnp.float32))
    square_sum = jnp.sum(jnp.sum(acc, axis=0, keepdims=True), axis=1, keepdims=True)
    root_mean = jnp.sqrt(jnp.maximum(square_sum, 0.0) / 786432.0 + 1e-06)
    fetch.wait()
    left = jnp.where(lax.broadcasted_iota(jnp.int32, (16, N), 0) == 0, wide, 0.0).astype(jnp.bfloat16)
    direction = jnp.dot(left, held[...], preferred_element_type=jnp.float32)
    out_ref[...] = -direction[0:1, :] / root_mean


def solve_call(gram, energy, centred):
    width = centred.shape[1]
    return pl.pallas_call(
        solve_kernel,
        out_shape=jax.ShapeDtypeStruct((1, width), jnp.float32),
        in_specs=[pl.BlockSpec(memory_space=pltpu.VMEM), pl.BlockSpec(memory_space=pltpu.VMEM), pl.BlockSpec(memory_space=pl.ANY)],
        out_specs=pl.BlockSpec(memory_space=pltpu.VMEM),
        scratch_shapes=[
            pltpu.VMEM((N + GR, N), jnp.float32),
            pltpu.VMEM((N, width), jnp.bfloat16),
            pltpu.VMEM((GR, N), jnp.float32),
            pltpu.VMEM((N, NB), jnp.float32),
            pltpu.SemaphoreType.DMA,
        ],
        compiler_params=pltpu.CompilerParams(vmem_limit_bytes=48 * 1024 * 1024),
        name="solve",
    )(gram, energy, centred)


SITES = 100


def bond_weights():
    side = math.isqrt(SITES)
    site = lax.broadcasted_iota(jnp.int32, (SITES, SITES), 0)
    other = lax.broadcasted_iota(jnp.int32, (SITES, SITES), 1)
    row, col = site // side, site % side
    other_row, other_col = other // side, other % side

    def bond(down, right):
        return ((other_row == (row + down) % side) & (other_col == (col + right) % side)).astype(jnp.float32)

    return 0.25 * (bond(0, 1) + bond(1, 0)) + 0.125 * (bond(1, 1) + bond(1, -1))


def diagonal_energy(spin_bits):
    spin_signs = (2 * spin_bits - 1).astype(jnp.float32)
    return jnp.sum(jnp.dot(spin_signs, bond_weights(), preferred_element_type=jnp.float32) * spin_signs, axis=1)


def on_device(spin_bits, flip_energy, jacobian):
    energy = diagonal_energy(spin_bits) + flip_energy
    first = (lax.axis_index("par") == 0).astype(jnp.float32)
    place = lax.axis_index("samp") * energy.shape[0]
    energy_rows = lax.dynamic_update_slice(jnp.zeros((GR, N), jnp.float32), (energy * first)[None, :], (0, place))
    columns = lax.all_to_all(jacobian, "samp", split_axis=1, concat_axis=0, tiled=True)
    column_mean = jnp.sum(columns, axis=0, dtype=jnp.float32) / N
    centred = (columns.astype(jnp.float32) - column_mean[None, :]).astype(jnp.bfloat16)
    part_gram = lax.dot_general(
        centred, centred, (((1,), (1,)), ((), ())), preferred_element_type=jnp.float32
    )
    total = lax.psum(jnp.concatenate([part_gram, energy_rows], axis=0), ("samp", "par"))
    return solve_call(total[:N], total[N:N + 1], centred).reshape(1, 1, -1)


def solution(mesh):
    return jax.shard_map(
        on_device,
        mesh=mesh,
        in_specs=(P("samp", None), P("samp"), P("samp", "par")),
        out_specs=P("par", "samp", None),
        check_vma=False,
    )
```

```python
import math

import jax
import jax.numpy as jnp
from jax import lax
from jax.experimental import pallas as pl
from jax.experimental.pallas import tpu as pltpu
from jax.sharding import PartitionSpec as P

SITES = 100
N = 1024
NB = 128
GR = 8
BLOCKS = N // NB
PARAMS = 786432
PER = 16
WIDTH = 3072
PIECES = 4
PIECE = WIDTH // PIECES
PACKED = BLOCKS * (BLOCKS + 1) // 2 * NB
HALF = PACKED // 2
ROWS_ONE = HALF // 4
ROWS_TWO = ROWS_ONE // 4
ROWS_LAST = 16
MESH = pl.DeviceIdType.MESH


def block_at(i, j):
    start = (i * (i + 1) // 2 + j) * NB
    return slice(start, start + NB)


def bond_weights():
    side = math.isqrt(SITES)
    site = lax.broadcasted_iota(jnp.int32, (SITES, SITES), 0)
    other = lax.broadcasted_iota(jnp.int32, (SITES, SITES), 1)
    row, col = site // side, site % side
    other_row, other_col = other // side, other % side

    def bond(down, right):
        hit = (other_row == (row + down) % side) & (other_col == (col + right + side) % side)
        return jnp.where(hit, 1.0, 0.0)

    return 0.25 * (bond(0, 1) + bond(1, 0)) + 0.125 * (bond(1, 1) + bond(1, -1))


def gram_kernel(
    spin_ref, bond_ref, flip_ref, jac_ref,
    gram_ref, energy_ref, centred_ref,
    held, packed, final, tiles, slot_core, slot_one, slot_two, slot_last,
    send_sem, recv_sem, own_sem, tile_send, tile_recv, out_sem, sum_send, sum_recv,
):
    samp, par = lax.axis_index("samp"), lax.axis_index("par")
    core = par % 2
    x_hi, y, z = samp // 32, (samp // 8) % 4, samp % 8
    x = x_hi * 2 + par // 2

    def device(x_at, y_at, z_at, core_at):
        return {"samp": (x_at // 2) * 32 + y_at * 8 + z_at, "par": (x_at % 2) * 2 + core_at}

    barrier = pltpu.get_barrier_semaphore()

    def greet(step, carry):
        pl.semaphore_signal(
            barrier, inc=1, device_id={"samp": lax.rem(samp + step, 64), "par": par}, device_id_type=MESH
        )
        return carry

    lax.fori_loop(1, 64, greet, 0)
    for partner in (device(x, y, z, 1 - core), device((x + 1) % 4, y, z, core), device((x + 3) % 4, y, z, core)):
        pl.semaphore_signal(barrier, inc=1, device_id=partner, device_id_type=MESH)

    mine = pl.ds(pl.multiple_of(samp * PER, PER), PER)
    own = pltpu.make_async_copy(
        jac_ref.at[:, pl.ds(pl.multiple_of(samp * WIDTH, NB), WIDTH)], held.at[mine], own_sem
    )
    own.start()

    signs = (2 * spin_ref[...] - 1).astype(jnp.float32).astype(jnp.bfloat16)
    linked = jnp.dot(signs, bond_ref[...], preferred_element_type=jnp.float32)
    bonds = jnp.sum(linked * signs.astype(jnp.float32), axis=1, keepdims=True)
    values = bonds + flip_ref[...]
    lane = lax.broadcasted_iota(jnp.int32, (PER, NB), 1)
    sample = lax.broadcasted_iota(jnp.int32, (PER, NB), 0)
    line = jnp.sum(jnp.where(lane == sample + (samp % 8) * PER, values, 0.0), axis=0, keepdims=True)
    sub = lax.broadcasted_iota(jnp.int32, (GR, NB), 0)
    tile_at = pl.ds(pl.multiple_of(samp * GR, GR), GR)
    tiles[tile_at, :] = jnp.where(sub == samp // 8, line, 0.0)

    pl.semaphore_wait(barrier, 66)

    def send_tile(step, carry):
        pltpu.make_async_remote_copy(
            src_ref=tiles.at[tile_at],
            dst_ref=tiles.at[tile_at],
            send_sem=tile_send,
            recv_sem=tile_recv,
            device_id={"samp": lax.rem(samp + step, 64), "par": par},
            device_id_type=MESH,
        ).start()
        return carry

    def send_block(piece, x_to, y_to, z_to):
        to = x_to * 32 + y_to * 8 + z_to
        pltpu.make_async_remote_copy(
            src_ref=jac_ref.at[:, pl.ds(pl.multiple_of(to * WIDTH + piece * PIECE, NB), PIECE)],
            dst_ref=held.at[mine, pl.ds(pl.multiple_of(piece * PIECE, NB), PIECE)],
            send_sem=send_sem,
            recv_sem=recv_sem.at[piece],
            device_id={"samp": to, "par": par},
            device_id_type=MESH,
        ).start()

    def send_plane(step, carry):
        piece, plane = step // 8, step % 8
        x_to = (x_hi + 1 - plane // 4) % 2
        y_to = (y + 6 - plane % 4) % 4
        for z_off in (4, 7, 3, 5, 2, 6, 1):
            send_block(piece, x_to, y_to, (z + z_off) % 8)

        @pl.when(plane != 6)
        def _():
            send_block(piece, x_to, y_to, z)

        return carry

    lax.fori_loop(0, 8 * PIECES, send_plane, 0)
    lax.fori_loop(1, 64, send_tile, 0)
    own.wait()
    packed[...] = jnp.zeros_like(packed)

    def work_piece(piece, carry):
        cols = pl.ds(pl.multiple_of(piece * PIECE, NB), PIECE)
        others = held.at[pl.ds(0, N - PER), cols]
        pltpu.make_async_copy(others, others, recv_sem.at[piece]).wait()

        def add_rows(i, total):
            return total + held[pl.ds(pl.multiple_of(i * PER, PER), PER), cols].astype(jnp.float32)

        total = lax.fori_loop(0, N // PER, add_rows, jnp.zeros((PER, PIECE), jnp.float32), unroll=4)
        mean = jnp.sum(total, axis=0, keepdims=True) * (1.0 / N)

        def centre_rows(i, carry):
            at = pl.ds(pl.multiple_of(i * PER, PER), PER)
            held[at, cols] = (held[at, cols].astype(jnp.float32) - mean).astype(jnp.bfloat16)
            return carry

        lax.fori_loop(0, N // PER, centre_rows, 0, unroll=4)
        pltpu.make_async_copy(held.at[:, cols], centred_ref.at[:, cols], out_sem.at[piece]).start()
        for i in range(0, BLOCKS, 2):
            size = (i + 2) * NB
            product = lax.dot_general(
                held[i * NB:size, cols], held[0:size, cols], (((1,), (1,)), ((), ())),
                preferred_element_type=jnp.float32,
            )
            for r in range(2):
                for j in range(i + r + 1):
                    at = block_at(i + r, j)
                    packed[at, :] = packed[at, :] + product[r * NB:(r + 1) * NB, j * NB:(j + 1) * NB]
        return carry

    lax.fori_loop(0, PIECES, work_piece, 0)

    x_or_y = (x, y)
    pos_one = x_or_y[0] + core * (y - x)
    pos_two = x_or_y[1] + core * (x - y)

    def on_one(at):
        return device(at + core * (x - at), y + core * (at - y), z, core)

    def on_two(at):
        return device(x + core * (at - x), at + core * (y - at), z, core)

    def rows(start, size):
        return pl.ds(pl.multiple_of(start, GR), size)

    def send(stage, source, target, to):
        pltpu.make_async_remote_copy(
            src_ref=source, dst_ref=target, send_sem=sum_send.at[stage], recv_sem=sum_recv.at[stage],
            device_id=to, device_id_type=MESH,
        ).start()

    def arrived(stage, like):
        pltpu.make_async_copy(like, like, sum_recv.at[stage]).wait()

    def left(stage, like):
        pltpu.make_async_copy(like, like, sum_send.at[stage]).wait()

    half = core * HALF
    send(0, packed.at[rows((1 - core) * HALF, HALF)], slot_core, device(x, y, z, 1 - core))
    arrived(0, slot_core)
    packed[rows(half, HALF), :] = packed[rows(half, HALF), :] + slot_core[...]

    for step in (2, 1, 3):
        to = (pos_one + step) % 4
        send(1, packed.at[rows(half + to * ROWS_ONE, ROWS_ONE)], slot_one.at[pos_one], on_one(to))
    arrived(1, slot_one.at[pl.ds(0, 3)])
    one = half + pos_one * ROWS_ONE
    packed[rows(one, ROWS_ONE), :] = (packed[rows(one, ROWS_ONE), :] + slot_one[(pos_one + 1) % 4]) + (
        slot_one[(pos_one + 2) % 4] + slot_one[(pos_one + 3) % 4]
    )

    for step in (2, 1, 3):
        to = (pos_two + step) % 4
        send(2, packed.at[rows(one + to * ROWS_TWO, ROWS_TWO)], slot_two.at[pos_two], on_two(to))
    arrived(2, slot_two.at[pl.ds(0, 3)])
    two = one + pos_two * ROWS_TWO
    packed[rows(two, ROWS_TWO), :] = (packed[rows(two, ROWS_TWO), :] + slot_two[(pos_two + 1) % 4]) + (
        slot_two[(pos_two + 2) % 4] + slot_two[(pos_two + 3) % 4]
    )

    spare = rows(two + 8 * ROWS_LAST, ROWS_LAST)
    for step in (4, 3, 5, 2, 6, 1, 7):
        to = (z + step) % 8
        send(3, packed.at[rows(two + to * ROWS_LAST, ROWS_LAST)], slot_last.at[z, 0:ROWS_LAST], device(x, y, to, core))
        send(3, packed.at[spare], slot_last.at[z, ROWS_LAST:2 * ROWS_LAST], device(x, y, to, core))
    last = rows(two + z * ROWS_LAST, ROWS_LAST)
    slot_last[z, 0:ROWS_LAST] = packed[last, :]
    slot_last[z, ROWS_LAST:2 * ROWS_LAST] = packed[spare, :]
    arrived(3, slot_last.at[pl.ds(0, 7)])
    total = slot_last[0]
    for i in range(1, 8):
        total = total + slot_last[i]
    final[last, :] = total[0:ROWS_LAST]
    final[spare, :] = total[ROWS_LAST:2 * ROWS_LAST]

    for step in (4, 3, 5, 2, 6, 1, 7):
        send(4, final.at[last], final.at[last], device(x, y, (z + step) % 8, core))
    arrived(4, final.at[pl.ds(0, 7 * ROWS_LAST)])
    part = rows(two, ROWS_TWO)
    for step in (2, 1, 3):
        send(5, final.at[part], final.at[part], on_two((pos_two + step) % 4))
    arrived(5, final.at[pl.ds(0, 3 * ROWS_TWO)])
    part = rows(one, ROWS_ONE)
    for step in (2, 1, 3):
        send(6, final.at[part], final.at[part], on_one((pos_one + step) % 4))
    arrived(6, final.at[pl.ds(0, 3 * ROWS_ONE)])
    part = rows(half, HALF)
    send(7, final.at[part], final.at[part], device(x, y, z, 1 - core))

    others = tiles.at[pl.ds(0, 63 * GR)]
    pltpu.make_async_copy(others, others, tile_recv).wait()
    energy = tiles[0:GR, :]
    for i in range(1, 64):
        energy = energy + tiles[i * GR:(i + 1) * GR, :]
    energy_ref[...] = energy

    arrived(7, final.at[pl.ds(0, HALF)])
    result = pltpu.make_async_copy(final, gram_ref, own_sem)
    result.start()

    for piece in range(PIECES):
        cols = pl.ds(piece * PIECE, PIECE)
        pltpu.make_async_copy(held.at[:, cols], centred_ref.at[:, cols], out_sem.at[piece]).wait()
    others = held.at[pl.ds(0, N - PER)]
    pltpu.make_async_copy(others, others, send_sem).wait()
    others = tiles.at[pl.ds(0, 63 * GR)]
    pltpu.make_async_copy(others, others, tile_send).wait()
    left(0, slot_core)
    left(1, slot_one.at[pl.ds(0, 3)])
    left(2, slot_two.at[pl.ds(0, 3)])
    left(3, slot_last.at[pl.ds(0, 7)])
    left(4, final.at[pl.ds(0, 7 * ROWS_LAST)])
    left(5, final.at[pl.ds(0, 3 * ROWS_TWO)])
    left(6, final.at[pl.ds(0, 3 * ROWS_ONE)])
    left(7, final.at[pl.ds(0, HALF)])
    result.wait()


def gram_call(spin_bits, flip_energy, jacobian):
    vmem = pl.BlockSpec(memory_space=pltpu.VMEM)
    anywhere = pl.BlockSpec(memory_space=pl.ANY)
    return pl.pallas_call(
        gram_kernel,
        out_shape=(
            jax.ShapeDtypeStruct((PACKED, NB), jnp.float32),
            jax.ShapeDtypeStruct((GR, NB), jnp.float32),
            jax.ShapeDtypeStruct((N, WIDTH), jnp.bfloat16),
        ),
        in_specs=[vmem, vmem, vmem, anywhere],
        out_specs=(anywhere, vmem, anywhere),
        scratch_shapes=[
            pltpu.VMEM((N, WIDTH), jnp.bfloat16),
            pltpu.VMEM((PACKED, NB), jnp.float32),
            pltpu.VMEM((PACKED, NB), jnp.float32),
            pltpu.VMEM((64 * GR, NB), jnp.float32),
            pltpu.VMEM((HALF, NB), jnp.float32),
            pltpu.VMEM((4, ROWS_ONE, NB), jnp.float32),
            pltpu.VMEM((4, ROWS_TWO, NB), jnp.float32),
            pltpu.VMEM((8, 2 * ROWS_LAST, NB), jnp.float32),
            pltpu.SemaphoreType.DMA,
            pltpu.SemaphoreType.DMA((PIECES,)),
            pltpu.SemaphoreType.DMA,
            pltpu.SemaphoreType.DMA,
            pltpu.SemaphoreType.DMA,
            pltpu.SemaphoreType.DMA((PIECES,)),
            pltpu.SemaphoreType.DMA((8,)),
            pltpu.SemaphoreType.DMA((8,)),
        ],
        compiler_params=pltpu.CompilerParams(
            collective_id=0, has_side_effects=True, vmem_limit_bytes=48 * 1024 * 1024
        ),
        name="gram",
    )(spin_bits, bond_weights().astype(jnp.bfloat16), flip_energy.reshape(PER, 1), jacobian)


def split3(x):
    high = x.astype(jnp.bfloat16)
    rest = x - high.astype(jnp.float32)
    mid = rest.astype(jnp.bfloat16)
    low = (rest - mid.astype(jnp.float32)).astype(jnp.bfloat16)
    return high, mid, low


def dot_wide(a, b, turned=False):
    ah, am, al = split3(a)
    bh, bm, bl = split3(b)
    left = jnp.concatenate([ah, ah, am, am, ah, al], axis=1)
    right = jnp.concatenate([bh, bm, bh, bm, bl, bh], axis=1 if turned else 0)
    dims = (((1,), (1 if turned else 0,)), ((), ()))
    return lax.dot_general(left, right, dims, preferred_element_type=jnp.float32)


def lanes(v, c):
    return jnp.broadcast_to(v[:, c:c + 1], (GR, NB))


def subs(v, r):
    return jnp.broadcast_to(v[r:r + 1, :], (GR, NB))


def invert_block(rows):
    lane = lax.broadcasted_iota(jnp.int32, (GR, NB), 1)
    sub = lax.broadcasted_iota(jnp.int32, (GR, NB), 0)
    count = NB // GR
    for g in range(count):
        base = g * GR
        own = rows[g]
        piv_cols = [lanes(own, base + c) for c in range(GR)]
        in_piv = (lane >= base) & (lane < base + GR)
        row = jnp.where(in_piv, jnp.where(lane - base == sub, 1.0, 0.0), own)
        for q in range(GR):
            at = sub == q
            inv = 1.0 / subs(piv_cols[q], q)
            coef = jnp.where(at, -inv, piv_cols[q] * inv)
            row = jnp.where(at, 0.0, row) - coef * subs(row, q)
            for c in range(q + 1, GR):
                piv_cols[c] = jnp.where(at, 0.0, piv_cols[c]) - coef * subs(piv_cols[c], q)
        spread = [subs(row, q) for q in range(GR)]
        new_rows = []
        for v in range(count):
            if v == g:
                new_rows.append(row)
                continue
            terms = [lanes(rows[v], base + q) * spread[q] for q in range(GR)]
            total = (((terms[0] + terms[1]) + (terms[2] + terms[3]))
                     + ((terms[4] + terms[5]) + (terms[6] + terms[7])))
            new_rows.append(jnp.where(in_piv, 0.0, rows[v]) - total)
        rows = new_rows
    return rows


def solve_kernel(gram_ref, energy_ref, centred_ref, out_ref, work, held, x_row, x_col, sem):
    fetch = pltpu.make_async_copy(centred_ref, held, sem)
    fetch.start()
    sub = lax.broadcasted_iota(jnp.int32, (NB, NB), 0)
    lane = lax.broadcasted_iota(jnp.int32, (NB, NB), 1)
    eye = jnp.where(sub == lane, 1.0, 0.0)
    for i in range(BLOCKS):
        at = slice(i * NB, (i + 1) * NB)
        for j in range(i):
            work[at, j * NB:(j + 1) * NB] = gram_ref[block_at(i, j), :]
        work[at, at] = gram_ref[block_at(i, i), :] + 0.5 * eye
    tile = energy_ref[...]
    mean = jnp.sum(jnp.sum(tile, axis=1, keepdims=True), axis=0, keepdims=True) * (1.0 / N)
    tile = tile - mean
    for i in range(BLOCKS):
        work[N:N + GR, i * NB:(i + 1) * NB] = subs(tile, i)

    def stage(k, carry):
        at = pl.ds(pl.multiple_of(k * NB, NB), NB)
        rows = [work[pl.ds(pl.multiple_of(k * NB + v * GR, GR), GR), at] for v in range(NB // GR)]
        rows = invert_block(rows)
        for v in range(NB // GR):
            work[pl.ds(pl.multiple_of(k * NB + v * GR, GR), GR), at] = rows[v]
        for c in range(BLOCKS - 1):
            @pl.when(k == c)
            def _():
                own = slice(c * NB, (c + 1) * NB)
                after = slice((c + 1) * NB, N)
                below = slice((c + 1) * NB, N + GR)
                turned = dot_wide(work[own, own], work[after, own], turned=True)
                work[below, after] = work[below, after] - dot_wide(work[below, own], turned)
                work[own, after] = turned
        return carry

    lax.fori_loop(0, BLOCKS, stage, 0)

    for k in range(BLOCKS - 1, -1, -1):
        own = slice(k * NB, (k + 1) * NB)
        total = work[own, own] * work[N:N + 1, own]
        for j in range(k + 1, BLOCKS):
            col = slice(j * NB, (j + 1) * NB)
            total = total - work[own, col] * x_row[0:1, col]
        column = jnp.sum(total, axis=1, keepdims=True)
        column = jnp.broadcast_to(column, (NB, NB))
        x_row[0:1, own] = jnp.sum(column * eye, axis=0, keepdims=True)
        x_col[own, :] = column.astype(jnp.bfloat16).astype(jnp.float32)

    wide = x_row[0:1, :].astype(jnp.bfloat16).astype(jnp.float32)

    acc = jnp.zeros((NB, NB), jnp.float32)
    for i in range(BLOCKS):
        part = gram_ref[block_at(i, i), :] * (0.5 * wide[:, i * NB:(i + 1) * NB])
        for j in range(i):
            part = part + gram_ref[block_at(i, j), :] * wide[:, j * NB:(j + 1) * NB]
        acc = acc + part * x_col[i * NB:(i + 1) * NB, :]
    square_sum = 2.0 * jnp.sum(jnp.sum(acc, axis=0, keepdims=True), axis=1, keepdims=True)
    root_mean = jnp.sqrt(jnp.maximum(square_sum, 0.0) / PARAMS + 1e-06)
    fetch.wait()
    left = jnp.where(lax.broadcasted_iota(jnp.int32, (PER, N), 0) == 0, wide, 0.0).astype(jnp.bfloat16)
    direction = jnp.dot(left, held[...], preferred_element_type=jnp.float32)
    out_ref[...] = -direction[0:1, :] / root_mean


def solve_call(gram, energy, centred):
    vmem = pl.BlockSpec(memory_space=pltpu.VMEM)
    return pl.pallas_call(
        solve_kernel,
        out_shape=jax.ShapeDtypeStruct((1, WIDTH), jnp.float32),
        in_specs=[vmem, vmem, pl.BlockSpec(memory_space=pl.ANY)],
        out_specs=vmem,
        scratch_shapes=[
            pltpu.VMEM((N + GR, N), jnp.float32),
            pltpu.VMEM((N, WIDTH), jnp.bfloat16),
            pltpu.VMEM((GR, N), jnp.float32),
            pltpu.VMEM((N, NB), jnp.float32),
            pltpu.SemaphoreType.DMA,
        ],
        compiler_params=pltpu.CompilerParams(vmem_limit_bytes=48 * 1024 * 1024),
        name="solve",
    )(gram, energy, centred)


def on_device(spin_bits, flip_energy, jacobian):
    gram, energy, centred = gram_call(spin_bits, flip_energy, jacobian)
    return solve_call(gram, energy, centred).reshape(1, 1, -1)


def solution(mesh):
    return jax.shard_map(
        on_device,
        mesh=mesh,
        in_specs=(P("samp", None), P("samp"), P("samp", "par")),
        out_specs=P("par", "samp", None),
        check_vma=False,
    )
```

```python
import math

import jax
import jax.numpy as jnp
from jax import lax
from jax.experimental import pallas as pl
from jax.experimental.pallas import tpu as pltpu
from jax.sharding import PartitionSpec as P

SITES = 100
N = 1024
NB = 128
GR = 8
BLOCKS = N // NB
PARAMS = 786432
PER = 16
WIDTH = 3072
PIECES = 4
PIECE = WIDTH // PIECES
PACKED = BLOCKS * (BLOCKS + 1) // 2 * NB
HALF = PACKED // 2
ROWS_CORE = HALF // 2
ROWS_ONE = ROWS_CORE // 4
ROWS_TWO = ROWS_ONE // 4
ROWS_LAST = 8
STEPS = 8
MESH = pl.DeviceIdType.MESH


def block_at(i, j):
    start = (j * BLOCKS - j * (j - 1) // 2 + i - j) * NB
    return slice(start, start + NB)


def bond_weights():
    side = math.isqrt(SITES)
    site = lax.broadcasted_iota(jnp.int32, (SITES, SITES), 0)
    other = lax.broadcasted_iota(jnp.int32, (SITES, SITES), 1)
    row = (site * 205) >> 11
    col = site - row * side

    def bond(down, right):
        to_row, to_col = row + down, col + right
        to_row = jnp.where(to_row >= side, to_row - side, to_row)
        to_col = jnp.where(to_col >= side, to_col - side, jnp.where(to_col < 0, to_col + side, to_col))
        return jnp.where(other == to_row * side + to_col, 1.0, 0.0)

    return 0.25 * (bond(0, 1) + bond(1, 0)) + 0.125 * (bond(1, 1) + bond(1, -1))


def sum_blocks(place, device, packed, final, slots, sum_send, sum_recv):
    x, y, z, core = place
    slot_core, slot_one, slot_two, slot_last, staged = slots
    pos_one = x + core * (y - x)
    pos_two = y + core * (x - y)
    other_core = device(x, y, z, 1 - core)

    def on_one(at):
        return device(at + core * (x - at), y + core * (at - y), z, core)

    def on_two(at):
        return device(x + core * (at - x), at + core * (y - at), z, core)

    def rows(start, size):
        return pl.ds(pl.multiple_of(start, GR), size)

    def send(part, step, source, target, to):
        at = part * STEPS + step
        pltpu.make_async_remote_copy(
            src_ref=source, dst_ref=target, send_sem=sum_send.at[at], recv_sem=sum_recv.at[at],
            device_id=to, device_id_type=MESH,
        ).start()

    def likes(part):
        return (
            slot_core.at[part],
            slot_one.at[part, pl.ds(0, 3)],
            slot_two.at[part, pl.ds(0, 3)],
            slot_last.at[part, pl.ds(0, 7)],
            final.at[pl.ds(0, 7 * ROWS_LAST)],
            final.at[pl.ds(0, 3 * ROWS_TWO)],
            final.at[pl.ds(0, 3 * ROWS_ONE)],
            final.at[pl.ds(0, ROWS_CORE)],
        )

    def arrived(part, step):
        like = likes(part)[step]
        pltpu.make_async_copy(like, like, sum_recv.at[part * STEPS + step]).wait()

    def starts(part):
        half = part * HALF + core * ROWS_CORE
        one = half + pos_one * ROWS_ONE
        return half, one, one + pos_two * ROWS_TWO

    def to_core(part):
        source = packed.at[rows(part * HALF + (1 - core) * ROWS_CORE, ROWS_CORE)]
        send(part, 0, source, slot_core.at[part], other_core)

    def to_one(part):
        half, one, two = starts(part)
        arrived(part, 0)
        packed[rows(half, ROWS_CORE), :] = packed[rows(half, ROWS_CORE), :] + slot_core[part]
        for step in (2, 1, 3):
            to = (pos_one + step) % 4
            send(part, 1, packed.at[rows(half + to * ROWS_ONE, ROWS_ONE)], slot_one.at[part, pos_one], on_one(to))

    def add_three(start, size, slot, part, pos):
        at = rows(start, size)
        packed[at, :] = (packed[at, :] + slot[part, (pos + 1) % 4]) + (
            slot[part, (pos + 2) % 4] + slot[part, (pos + 3) % 4]
        )

    def to_two(part):
        half, one, two = starts(part)
        arrived(part, 1)
        add_three(one, ROWS_ONE, slot_one, part, pos_one)
        for step in (2, 1, 3):
            to = (pos_two + step) % 4
            send(part, 2, packed.at[rows(one + to * ROWS_TWO, ROWS_TWO)], slot_two.at[part, pos_two], on_two(to))

    def to_last(part):
        half, one, two = starts(part)
        arrived(part, 2)
        add_three(two, ROWS_TWO, slot_two, part, pos_two)
        spare = packed[rows(two + 8 * ROWS_LAST, ROWS_LAST), :]
        for i in range(8):
            staged[part, i, 0:ROWS_LAST] = packed[rows(two + i * ROWS_LAST, ROWS_LAST), :]
            staged[part, i, ROWS_LAST:2 * ROWS_LAST] = spare
        for step in (4, 3, 5, 2, 6, 1, 7):
            to = (z + step) % 8
            send(part, 3, staged.at[part, to], slot_last.at[part, z], device(x, y, to, core))

    def back_last(part):
        half, one, two = starts(part)
        slot_last[part, z] = staged[part, z]
        arrived(part, 3)
        total = slot_last[part, 0]
        for i in range(1, 8):
            total = total + slot_last[part, i]
        last = rows(two + z * ROWS_LAST, ROWS_LAST)
        final[last, :] = total[0:ROWS_LAST]
        final[rows(two + 8 * ROWS_LAST, ROWS_LAST), :] = total[ROWS_LAST:2 * ROWS_LAST]
        for step in (4, 3, 5, 2, 6, 1, 7):
            send(part, 4, final.at[last], final.at[last], device(x, y, (z + step) % 8, core))

    def back_two(part):
        half, one, two = starts(part)
        arrived(part, 4)
        for step in (2, 1, 3):
            own = final.at[rows(two, ROWS_TWO)]
            send(part, 5, own, own, on_two((pos_two + step) % 4))

    def back_one(part):
        half, one, two = starts(part)
        arrived(part, 5)
        for step in (2, 1, 3):
            own = final.at[rows(one, ROWS_ONE)]
            send(part, 6, own, own, on_one((pos_one + step) % 4))

    def back_core(part):
        half, one, two = starts(part)
        arrived(part, 6)
        own = final.at[rows(half, ROWS_CORE)]
        send(part, 7, own, own, other_core)

    for move in (to_core, to_one, to_two, to_last, back_last, back_two, back_one, back_core):
        for part in range(2):
            move(part)

    def finish():
        for part in range(2):
            arrived(part, 7)
            for step in range(STEPS):
                like = likes(part)[step]
                pltpu.make_async_copy(like, like, sum_send.at[part * STEPS + step]).wait()

    return finish


def gram_kernel(
    spin_ref, flip_ref, jac_ref,
    gram_ref, energy_ref, centred_ref,
    held, packed, final, tiles, slot_core, slot_one, slot_two, slot_last, staged,
    send_sem, recv_sem, own_sem, tile_send, tile_recv, out_sem, sum_send, sum_recv,
):
    samp, par = lax.axis_index("samp"), lax.axis_index("par")
    core = par % 2
    x_hi, y, z = samp // 32, (samp // 8) % 4, samp % 8
    x = x_hi * 2 + par // 2

    def device(x_at, y_at, z_at, core_at):
        return {"samp": (x_at // 2) * 32 + y_at * 8 + z_at, "par": (x_at % 2) * 2 + core_at}

    barrier = pltpu.get_barrier_semaphore()

    def greet(step, carry):
        pl.semaphore_signal(
            barrier, inc=1, device_id={"samp": lax.rem(samp + step, 64), "par": par}, device_id_type=MESH
        )
        return carry

    lax.fori_loop(1, 64, greet, 0)
    for partner in (device(x, y, z, 1 - core), device((x + 1) % 4, y, z, core), device((x + 3) % 4, y, z, core)):
        pl.semaphore_signal(barrier, inc=1, device_id=partner, device_id_type=MESH)

    mine = pl.ds(pl.multiple_of(samp * PER, PER), PER)
    own = pltpu.make_async_copy(
        jac_ref.at[:, pl.ds(pl.multiple_of(samp * WIDTH, NB), WIDTH)], held.at[mine], own_sem
    )
    own.start()

    signs = (2 * spin_ref[...] - 1).astype(jnp.float32).astype(jnp.bfloat16)
    linked = jnp.dot(signs, bond_weights().astype(jnp.bfloat16), preferred_element_type=jnp.float32)
    bonds = jnp.sum(linked * signs.astype(jnp.float32), axis=1, keepdims=True)
    square = (PER, PER)
    same = lax.broadcasted_iota(jnp.int32, square, 0) == lax.broadcasted_iota(jnp.int32, square, 1)
    values = bonds + jnp.sum(jnp.where(same, flip_ref[...], 0.0), axis=1, keepdims=True)
    lane = lax.broadcasted_iota(jnp.int32, (PER, NB), 1)
    sample = lax.broadcasted_iota(jnp.int32, (PER, NB), 0)
    line = jnp.sum(jnp.where(lane == sample + (samp % 8) * PER, values, 0.0), axis=0, keepdims=True)
    sub = lax.broadcasted_iota(jnp.int32, (GR, NB), 0)
    tile_at = pl.ds(pl.multiple_of(samp * GR, GR), GR)
    tiles[tile_at, :] = jnp.where(sub == samp // 8, line, 0.0)

    pl.semaphore_wait(barrier, 66)

    def send_tile(step, carry):
        pltpu.make_async_remote_copy(
            src_ref=tiles.at[tile_at],
            dst_ref=tiles.at[tile_at],
            send_sem=tile_send,
            recv_sem=tile_recv,
            device_id={"samp": lax.rem(samp + step, 64), "par": par},
            device_id_type=MESH,
        ).start()
        return carry

    def send_block(piece, x_to, y_to, z_to):
        to = x_to * 32 + y_to * 8 + z_to
        pltpu.make_async_remote_copy(
            src_ref=jac_ref.at[:, pl.ds(pl.multiple_of(to * WIDTH + piece * PIECE, NB), PIECE)],
            dst_ref=held.at[mine, pl.ds(pl.multiple_of(piece * PIECE, NB), PIECE)],
            send_sem=send_sem,
            recv_sem=recv_sem.at[piece],
            device_id={"samp": to, "par": par},
            device_id_type=MESH,
        ).start()

    def send_plane(step, carry):
        piece, plane = step // 8, step % 8
        x_to = (x_hi + 1 - plane // 4) % 2
        y_to = (y + 6 - plane % 4) % 4
        for z_off in (4, 7, 3, 5, 2, 6, 1):
            send_block(piece, x_to, y_to, (z + z_off) % 8)

        @pl.when(plane != 6)
        def _():
            send_block(piece, x_to, y_to, z)

        return carry

    lax.fori_loop(0, 8 * PIECES, send_plane, 0)
    lax.fori_loop(1, 64, send_tile, 0)
    own.wait()
    packed[...] = jnp.zeros_like(packed)

    def work_piece(piece, carry):
        cols = pl.ds(pl.multiple_of(piece * PIECE, NB), PIECE)
        others = held.at[pl.ds(0, N - PER), cols]
        pltpu.make_async_copy(others, others, recv_sem.at[piece]).wait()

        def add_rows(i, total):
            return total + held[pl.ds(pl.multiple_of(i * PER, PER), PER), cols].astype(jnp.float32)

        total = lax.fori_loop(0, N // PER, add_rows, jnp.zeros((PER, PIECE), jnp.float32), unroll=4)
        mean = jnp.sum(total, axis=0, keepdims=True) * (1.0 / N)

        def centre_rows(i, carry):
            at = pl.ds(pl.multiple_of(i * PER, PER), PER)
            held[at, cols] = (held[at, cols].astype(jnp.float32) - mean).astype(jnp.bfloat16)
            return carry

        lax.fori_loop(0, N // PER, centre_rows, 0, unroll=4)
        pltpu.make_async_copy(held.at[:, cols], centred_ref.at[:, cols], out_sem.at[piece]).start()
        for i in range(0, BLOCKS, 2):
            size = (i + 2) * NB
            product = lax.dot_general(
                held[i * NB:size, cols], held[0:size, cols], (((1,), (1,)), ((), ())),
                preferred_element_type=jnp.float32,
            )
            for r in range(2):
                for j in range(i + r + 1):
                    at = block_at(i + r, j)
                    packed[at, :] = packed[at, :] + product[r * NB:(r + 1) * NB, j * NB:(j + 1) * NB]
        return carry

    lax.fori_loop(0, PIECES, work_piece, 0)

    slots = (slot_core, slot_one, slot_two, slot_last, staged)
    finish = sum_blocks((x, y, z, core), device, packed, final, slots, sum_send, sum_recv)

    others = tiles.at[pl.ds(0, 63 * GR)]
    pltpu.make_async_copy(others, others, tile_recv).wait()
    energy = tiles[0:GR, :]
    for i in range(1, 64):
        energy = energy + tiles[i * GR:(i + 1) * GR, :]
    energy_ref[...] = energy

    finish()
    result = pltpu.make_async_copy(final, gram_ref, own_sem)
    result.start()

    for piece in range(PIECES):
        cols = pl.ds(piece * PIECE, PIECE)
        pltpu.make_async_copy(held.at[:, cols], centred_ref.at[:, cols], out_sem.at[piece]).wait()
    others = held.at[pl.ds(0, N - PER)]
    pltpu.make_async_copy(others, others, send_sem).wait()
    others = tiles.at[pl.ds(0, 63 * GR)]
    pltpu.make_async_copy(others, others, tile_send).wait()
    result.wait()


def gram_call(spin_bits, flip_energy, jacobian):
    vmem = pl.BlockSpec(memory_space=pltpu.VMEM)
    anywhere = pl.BlockSpec(memory_space=pl.ANY)
    return pl.pallas_call(
        gram_kernel,
        out_shape=(
            jax.ShapeDtypeStruct((PACKED, NB), jnp.float32),
            jax.ShapeDtypeStruct((GR, NB), jnp.float32),
            jax.ShapeDtypeStruct((N, WIDTH), jnp.bfloat16),
        ),
        in_specs=[vmem, vmem, anywhere],
        out_specs=(anywhere, vmem, anywhere),
        scratch_shapes=[
            pltpu.VMEM((N, WIDTH), jnp.bfloat16),
            pltpu.VMEM((PACKED, NB), jnp.float32),
            pltpu.VMEM((PACKED, NB), jnp.float32),
            pltpu.VMEM((64 * GR, NB), jnp.float32),
            pltpu.VMEM((2, ROWS_CORE, NB), jnp.float32),
            pltpu.VMEM((2, 4, ROWS_ONE, NB), jnp.float32),
            pltpu.VMEM((2, 4, ROWS_TWO, NB), jnp.float32),
            pltpu.VMEM((2, 8, 2 * ROWS_LAST, NB), jnp.float32),
            pltpu.VMEM((2, 8, 2 * ROWS_LAST, NB), jnp.float32),
            pltpu.SemaphoreType.DMA,
            pltpu.SemaphoreType.DMA((PIECES,)),
            pltpu.SemaphoreType.DMA,
            pltpu.SemaphoreType.DMA,
            pltpu.SemaphoreType.DMA,
            pltpu.SemaphoreType.DMA((PIECES,)),
            pltpu.SemaphoreType.DMA((2 * STEPS,)),
            pltpu.SemaphoreType.DMA((2 * STEPS,)),
        ],
        compiler_params=pltpu.CompilerParams(
            collective_id=0, has_side_effects=True, vmem_limit_bytes=48 * 1024 * 1024
        ),
        name="gram",
    )(spin_bits, flip_energy.reshape(1, PER), jacobian)


def split3(x):
    high = x.astype(jnp.bfloat16)
    rest = x - high.astype(jnp.float32)
    mid = rest.astype(jnp.bfloat16)
    low = (rest - mid.astype(jnp.float32)).astype(jnp.bfloat16)
    return high, mid, low


def dot_wide(a, b, turned=False):
    ah, am, al = split3(a)
    bh, bm, bl = split3(b)
    left = jnp.concatenate([ah, ah, am, am, ah, al], axis=1)
    right = jnp.concatenate([bh, bm, bh, bm, bl, bh], axis=1 if turned else 0)
    dims = (((1,), (1 if turned else 0,)), ((), ()))
    return lax.dot_general(left, right, dims, preferred_element_type=jnp.float32)


def lanes(v, c):
    return jnp.broadcast_to(v[:, c:c + 1], (GR, NB))


def subs(v, r):
    return jnp.broadcast_to(v[r:r + 1, :], (GR, NB))


def invert_block(rows):
    lane = lax.broadcasted_iota(jnp.int32, (GR, NB), 1)
    sub = lax.broadcasted_iota(jnp.int32, (GR, NB), 0)
    count = NB // GR
    for g in range(count):
        base = g * GR
        own = rows[g]
        piv_cols = [lanes(own, base + c) for c in range(GR)]
        in_piv = (lane >= base) & (lane < base + GR)
        row = jnp.where(in_piv, jnp.where(lane - base == sub, 1.0, 0.0), own)
        for q in range(GR):
            at = sub == q
            inv = 1.0 / subs(piv_cols[q], q)
            coef = jnp.where(at, -inv, piv_cols[q] * inv)
            row = jnp.where(at, 0.0, row) - coef * subs(row, q)
            for c in range(q + 1, GR):
                piv_cols[c] = jnp.where(at, 0.0, piv_cols[c]) - coef * subs(piv_cols[c], q)
        spread = [subs(row, q) for q in range(GR)]
        new_rows = []
        for v in range(count):
            if v == g:
                new_rows.append(row)
                continue
            terms = [lanes(rows[v], base + q) * spread[q] for q in range(GR)]
            total = (((terms[0] + terms[1]) + (terms[2] + terms[3]))
                     + ((terms[4] + terms[5]) + (terms[6] + terms[7])))
            new_rows.append(jnp.where(in_piv, 0.0, rows[v]) - total)
        rows = new_rows
    return rows


def solve_kernel(gram_ref, energy_ref, centred_ref, out_ref, work, held, x_row, x_col, sem):
    fetch = pltpu.make_async_copy(centred_ref, held, sem)
    fetch.start()
    sub = lax.broadcasted_iota(jnp.int32, (NB, NB), 0)
    lane = lax.broadcasted_iota(jnp.int32, (NB, NB), 1)
    eye = jnp.where(sub == lane, 1.0, 0.0)
    for i in range(BLOCKS):
        at = slice(i * NB, (i + 1) * NB)
        for j in range(i):
            work[at, j * NB:(j + 1) * NB] = gram_ref[block_at(i, j), :]
        work[at, at] = gram_ref[block_at(i, i), :] + 0.5 * eye
    tile = energy_ref[...]
    mean = jnp.sum(jnp.sum(tile, axis=1, keepdims=True), axis=0, keepdims=True) * (1.0 / N)
    tile = tile - mean
    for i in range(BLOCKS):
        work[N:N + GR, i * NB:(i + 1) * NB] = subs(tile, i)

    def stage(k, carry):
        at = pl.ds(pl.multiple_of(k * NB, NB), NB)
        rows = [work[pl.ds(pl.multiple_of(k * NB + v * GR, GR), GR), at] for v in range(NB // GR)]
        rows = invert_block(rows)
        for v in range(NB // GR):
            work[pl.ds(pl.multiple_of(k * NB + v * GR, GR), GR), at] = rows[v]
        for c in range(BLOCKS - 1):
            @pl.when(k == c)
            def _():
                own = slice(c * NB, (c + 1) * NB)
                after = slice((c + 1) * NB, N)
                below = slice((c + 1) * NB, N + GR)
                turned = dot_wide(work[own, own], work[after, own], turned=True)
                work[below, after] = work[below, after] - dot_wide(work[below, own], turned)
                work[own, after] = turned
        return carry

    lax.fori_loop(0, BLOCKS, stage, 0)

    for k in range(BLOCKS - 1, -1, -1):
        own = slice(k * NB, (k + 1) * NB)
        total = work[own, own] * work[N:N + 1, own]
        for j in range(k + 1, BLOCKS):
            col = slice(j * NB, (j + 1) * NB)
            total = total - work[own, col] * x_row[0:1, col]
        column = jnp.sum(total, axis=1, keepdims=True)
        column = jnp.broadcast_to(column, (NB, NB))
        x_row[0:1, own] = jnp.sum(column * eye, axis=0, keepdims=True)
        x_col[own, :] = column.astype(jnp.bfloat16).astype(jnp.float32)

    wide = x_row[0:1, :].astype(jnp.bfloat16).astype(jnp.float32)

    acc = jnp.zeros((NB, NB), jnp.float32)
    for i in range(BLOCKS):
        part = gram_ref[block_at(i, i), :] * (0.5 * wide[:, i * NB:(i + 1) * NB])
        for j in range(i):
            part = part + gram_ref[block_at(i, j), :] * wide[:, j * NB:(j + 1) * NB]
        acc = acc + part * x_col[i * NB:(i + 1) * NB, :]
    square_sum = 2.0 * jnp.sum(jnp.sum(acc, axis=0, keepdims=True), axis=1, keepdims=True)
    root_mean = jnp.sqrt(jnp.maximum(square_sum, 0.0) / PARAMS + 1e-06)
    fetch.wait()
    left = jnp.where(lax.broadcasted_iota(jnp.int32, (PER, N), 0) == 0, wide, 0.0).astype(jnp.bfloat16)
    direction = jnp.dot(left, held[...], preferred_element_type=jnp.float32)
    out_ref[...] = -direction[0:1, :] / root_mean


def solve_call(gram, energy, centred):
    vmem = pl.BlockSpec(memory_space=pltpu.VMEM)
    return pl.pallas_call(
        solve_kernel,
        out_shape=jax.ShapeDtypeStruct((1, WIDTH), jnp.float32),
        in_specs=[vmem, vmem, pl.BlockSpec(memory_space=pl.ANY)],
        out_specs=vmem,
        scratch_shapes=[
            pltpu.VMEM((N + GR, N), jnp.float32),
            pltpu.VMEM((N, WIDTH), jnp.bfloat16),
            pltpu.VMEM((GR, N), jnp.float32),
            pltpu.VMEM((N, NB), jnp.float32),
            pltpu.SemaphoreType.DMA,
        ],
        compiler_params=pltpu.CompilerParams(vmem_limit_bytes=48 * 1024 * 1024),
        name="solve",
    )(gram, energy, centred)


def on_device(spin_bits, flip_energy, jacobian):
    gram, energy, centred = gram_call(spin_bits, flip_energy, jacobian)
    return solve_call(gram, energy, centred).reshape(1, 1, -1)


def solution(mesh):
    return jax.shard_map(
        on_device,
        mesh=mesh,
        in_specs=(P("samp", None), P("samp"), P("samp", "par")),
        out_specs=P("par", "samp", None),
        check_vma=False,
    )
```

```python
import math

import jax
import jax.numpy as jnp
from jax import lax
from jax.experimental import pallas as pl
from jax.experimental.pallas import tpu as pltpu
from jax.sharding import PartitionSpec as P

SITES = 100
N = 1024
NB = 128
GR = 8
BLOCKS = N // NB
PARAMS = 786432
PER = 16
WIDTH = 3072
PIECES = 4
PIECE = WIDTH // PIECES
PACKED = BLOCKS * (BLOCKS + 1) // 2 * NB
HALF = PACKED // 2
ROWS_CORE = HALF // 2
ROWS_ONE = ROWS_CORE // 4
ROWS_TWO = ROWS_ONE // 4
ROWS_LAST = 8
STEPS = 8
MESH = pl.DeviceIdType.MESH


def block_at(i, j):
    start = (j * BLOCKS - j * (j - 1) // 2 + i - j) * NB
    return slice(start, start + NB)


def bond_weights():
    side = math.isqrt(SITES)
    site = lax.broadcasted_iota(jnp.int32, (SITES, SITES), 0)
    other = lax.broadcasted_iota(jnp.int32, (SITES, SITES), 1)
    row = (site * 205) >> 11
    col = site - row * side

    def bond(down, right):
        to_row, to_col = row + down, col + right
        to_row = jnp.where(to_row >= side, to_row - side, to_row)
        to_col = jnp.where(to_col >= side, to_col - side, jnp.where(to_col < 0, to_col + side, to_col))
        return jnp.where(other == to_row * side + to_col, 1.0, 0.0)

    return 0.25 * (bond(0, 1) + bond(1, 0)) + 0.125 * (bond(1, 1) + bond(1, -1))


def sum_blocks(place, device, packed, final, slots, sum_send, sum_recv):
    x, y, z, core = place
    slot_core, slot_one, slot_two, slot_last, staged = slots
    pos_one = x + core * (y - x)
    pos_two = y + core * (x - y)
    other_core = device(x, y, z, 1 - core)

    def on_one(at):
        return device(at + core * (x - at), y + core * (at - y), z, core)

    def on_two(at):
        return device(x + core * (at - x), at + core * (y - at), z, core)

    def rows(start, size):
        return pl.ds(pl.multiple_of(start, GR), size)

    def send(part, step, source, target, to):
        at = part * STEPS + step
        pltpu.make_async_remote_copy(
            src_ref=source, dst_ref=target, send_sem=sum_send.at[at], recv_sem=sum_recv.at[at],
            device_id=to, device_id_type=MESH,
        ).start()

    def likes(part):
        return (
            slot_core.at[part],
            slot_one.at[part, pl.ds(0, 3)],
            slot_two.at[part, pl.ds(0, 3)],
            slot_last.at[part, pl.ds(0, 7)],
            final.at[pl.ds(0, 7 * ROWS_LAST)],
            final.at[pl.ds(0, 3 * ROWS_TWO)],
            final.at[pl.ds(0, 3 * ROWS_ONE)],
            final.at[pl.ds(0, ROWS_CORE)],
        )

    def arrived(part, step):
        like = likes(part)[step]
        pltpu.make_async_copy(like, like, sum_recv.at[part * STEPS + step]).wait()

    def starts(part):
        half = part * HALF + core * ROWS_CORE
        one = half + pos_one * ROWS_ONE
        return half, one, one + pos_two * ROWS_TWO

    def to_core(part):
        source = packed.at[rows(part * HALF + (1 - core) * ROWS_CORE, ROWS_CORE)]
        send(part, 0, source, slot_core.at[part], other_core)

    def to_one(part):
        half, one, two = starts(part)
        arrived(part, 0)
        packed[rows(half, ROWS_CORE), :] = packed[rows(half, ROWS_CORE), :] + slot_core[part]
        for step in (2, 1, 3):
            to = (pos_one + step) % 4
            send(part, 1, packed.at[rows(half + to * ROWS_ONE, ROWS_ONE)], slot_one.at[part, pos_one], on_one(to))

    def add_three(start, size, slot, part, pos):
        at = rows(start, size)
        packed[at, :] = (packed[at, :] + slot[part, (pos + 1) % 4]) + (
            slot[part, (pos + 2) % 4] + slot[part, (pos + 3) % 4]
        )

    def to_two(part):
        half, one, two = starts(part)
        arrived(part, 1)
        add_three(one, ROWS_ONE, slot_one, part, pos_one)
        for step in (2, 1, 3):
            to = (pos_two + step) % 4
            send(part, 2, packed.at[rows(one + to * ROWS_TWO, ROWS_TWO)], slot_two.at[part, pos_two], on_two(to))

    def to_last(part):
        half, one, two = starts(part)
        arrived(part, 2)
        add_three(two, ROWS_TWO, slot_two, part, pos_two)
        spare = packed[rows(two + 8 * ROWS_LAST, ROWS_LAST), :]
        for i in range(8):
            staged[part, i, 0:ROWS_LAST] = packed[rows(two + i * ROWS_LAST, ROWS_LAST), :]
            staged[part, i, ROWS_LAST:2 * ROWS_LAST] = spare
        for step in (4, 3, 5, 2, 6, 1, 7):
            to = (z + step) % 8
            send(part, 3, staged.at[part, to], slot_last.at[part, z], device(x, y, to, core))

    def back_last(part):
        half, one, two = starts(part)
        slot_last[part, z] = staged[part, z]
        arrived(part, 3)
        total = slot_last[part, 0]
        for i in range(1, 8):
            total = total + slot_last[part, i]
        last = rows(two + z * ROWS_LAST, ROWS_LAST)
        final[last, :] = total[0:ROWS_LAST]
        final[rows(two + 8 * ROWS_LAST, ROWS_LAST), :] = total[ROWS_LAST:2 * ROWS_LAST]
        for step in (4, 3, 5, 2, 6, 1, 7):
            send(part, 4, final.at[last], final.at[last], device(x, y, (z + step) % 8, core))

    def back_two(part):
        half, one, two = starts(part)
        arrived(part, 4)
        for step in (2, 1, 3):
            own = final.at[rows(two, ROWS_TWO)]
            send(part, 5, own, own, on_two((pos_two + step) % 4))

    def back_one(part):
        half, one, two = starts(part)
        arrived(part, 5)
        for step in (2, 1, 3):
            own = final.at[rows(one, ROWS_ONE)]
            send(part, 6, own, own, on_one((pos_one + step) % 4))

    def back_core(part):
        half, one, two = starts(part)
        arrived(part, 6)
        own = final.at[rows(half, ROWS_CORE)]
        send(part, 7, own, own, other_core)

    for move in (to_core, to_one, to_two, to_last, back_last, back_two, back_one, back_core):
        for part in range(2):
            move(part)

    def finish():
        for part in range(2):
            arrived(part, 7)
            for step in range(STEPS):
                like = likes(part)[step]
                pltpu.make_async_copy(like, like, sum_send.at[part * STEPS + step]).wait()

    return finish


def gram_kernel(
    spin_ref, flip_ref, jac_ref,
    gram_ref, energy_ref, centred_ref,
    held, packed, final, tiles, slot_core, slot_one, slot_two, slot_last, staged,
    send_sem, recv_sem, own_sem, tile_send, tile_recv, out_sem, sum_send, sum_recv,
):
    samp, par = lax.axis_index("samp"), lax.axis_index("par")
    core = par % 2
    x_hi, y, z = samp // 32, (samp // 8) % 4, samp % 8
    x = x_hi * 2 + par // 2

    def device(x_at, y_at, z_at, core_at):
        return {"samp": (x_at // 2) * 32 + y_at * 8 + z_at, "par": (x_at % 2) * 2 + core_at}

    barrier = pltpu.get_barrier_semaphore()

    def greet(step, carry):
        pl.semaphore_signal(
            barrier, inc=1, device_id={"samp": lax.rem(samp + step, 64), "par": par}, device_id_type=MESH
        )
        return carry

    lax.fori_loop(1, 64, greet, 0)
    for partner in (device(x, y, z, 1 - core), device((x + 1) % 4, y, z, core), device((x + 3) % 4, y, z, core)):
        pl.semaphore_signal(barrier, inc=1, device_id=partner, device_id_type=MESH)

    mine = pl.ds(pl.multiple_of(samp * PER, PER), PER)
    own = pltpu.make_async_copy(
        jac_ref.at[:, pl.ds(pl.multiple_of(samp * WIDTH, NB), WIDTH)], held.at[mine], own_sem
    )
    own.start()

    signs = (2 * spin_ref[...] - 1).astype(jnp.float32).astype(jnp.bfloat16)
    linked = jnp.dot(signs, bond_weights().astype(jnp.bfloat16), preferred_element_type=jnp.float32)
    bonds = jnp.sum(linked * signs.astype(jnp.float32), axis=1, keepdims=True)
    square = (PER, PER)
    same = lax.broadcasted_iota(jnp.int32, square, 0) == lax.broadcasted_iota(jnp.int32, square, 1)
    values = bonds + jnp.sum(jnp.where(same, flip_ref[...], 0.0), axis=1, keepdims=True)
    lane = lax.broadcasted_iota(jnp.int32, (PER, NB), 1)
    sample = lax.broadcasted_iota(jnp.int32, (PER, NB), 0)
    line = jnp.sum(jnp.where(lane == sample + (samp % 8) * PER, values, 0.0), axis=0, keepdims=True)
    sub = lax.broadcasted_iota(jnp.int32, (GR, NB), 0)
    tile_at = pl.ds(pl.multiple_of(samp * GR, GR), GR)
    tiles[tile_at, :] = jnp.where(sub == samp // 8, line, 0.0)

    pl.semaphore_wait(barrier, 66)

    def send_tile(step, carry):
        pltpu.make_async_remote_copy(
            src_ref=tiles.at[tile_at],
            dst_ref=tiles.at[tile_at],
            send_sem=tile_send,
            recv_sem=tile_recv,
            device_id={"samp": lax.rem(samp + step, 64), "par": par},
            device_id_type=MESH,
        ).start()
        return carry

    def send_block(piece, x_to, y_to, z_to):
        to = x_to * 32 + y_to * 8 + z_to
        pltpu.make_async_remote_copy(
            src_ref=jac_ref.at[:, pl.ds(pl.multiple_of(to * WIDTH + piece * PIECE, NB), PIECE)],
            dst_ref=held.at[mine, pl.ds(pl.multiple_of(piece * PIECE, NB), PIECE)],
            send_sem=send_sem,
            recv_sem=recv_sem.at[piece],
            device_id={"samp": to, "par": par},
            device_id_type=MESH,
        ).start()

    def send_plane(step, carry):
        piece, plane = step // 8, step % 8
        x_to = (x_hi + 1 - plane // 4) % 2
        y_to = (y + 6 - plane % 4) % 4
        for z_off in (4, 7, 3, 5, 2, 6, 1):
            send_block(piece, x_to, y_to, (z + z_off) % 8)

        @pl.when(plane != 6)
        def _():
            send_block(piece, x_to, y_to, z)

        return carry

    lax.fori_loop(0, 8 * PIECES, send_plane, 0)
    lax.fori_loop(1, 64, send_tile, 0)
    own.wait()
    packed[...] = jnp.zeros_like(packed)

    def work_piece(piece, carry):
        cols = pl.ds(pl.multiple_of(piece * PIECE, NB), PIECE)
        others = held.at[pl.ds(0, N - PER), cols]
        pltpu.make_async_copy(others, others, recv_sem.at[piece]).wait()

        def add_rows(i, total):
            return total + held[pl.ds(pl.multiple_of(i * PER, PER), PER), cols].astype(jnp.float32)

        total = lax.fori_loop(0, N // PER, add_rows, jnp.zeros((PER, PIECE), jnp.float32), unroll=4)
        mean = jnp.sum(total, axis=0, keepdims=True) * (1.0 / N)

        def centre_rows(i, carry):
            at = pl.ds(pl.multiple_of(i * PER, PER), PER)
            held[at, cols] = (held[at, cols].astype(jnp.float32) - mean).astype(jnp.bfloat16)
            return carry

        lax.fori_loop(0, N // PER, centre_rows, 0, unroll=4)
        pltpu.make_async_copy(held.at[:, cols], centred_ref.at[:, cols], out_sem.at[piece]).start()
        for i in range(0, BLOCKS, 2):
            size = (i + 2) * NB
            product = lax.dot_general(
                held[i * NB:size, cols], held[0:size, cols], (((1,), (1,)), ((), ())),
                preferred_element_type=jnp.float32,
            )
            for r in range(2):
                for j in range(i + r + 1):
                    at = block_at(i + r, j)
                    packed[at, :] = packed[at, :] + product[r * NB:(r + 1) * NB, j * NB:(j + 1) * NB]
        return carry

    lax.fori_loop(0, PIECES, work_piece, 0)

    slots = (slot_core, slot_one, slot_two, slot_last, staged)
    finish = sum_blocks((x, y, z, core), device, packed, final, slots, sum_send, sum_recv)

    others = tiles.at[pl.ds(0, 63 * GR)]
    pltpu.make_async_copy(others, others, tile_recv).wait()
    energy = tiles[0:GR, :]
    for i in range(1, 64):
        energy = energy + tiles[i * GR:(i + 1) * GR, :]
    energy_ref[...] = energy

    finish()
    result = pltpu.make_async_copy(final, gram_ref, own_sem)
    result.start()

    for piece in range(PIECES):
        cols = pl.ds(piece * PIECE, PIECE)
        pltpu.make_async_copy(held.at[:, cols], centred_ref.at[:, cols], out_sem.at[piece]).wait()
    others = held.at[pl.ds(0, N - PER)]
    pltpu.make_async_copy(others, others, send_sem).wait()
    others = tiles.at[pl.ds(0, 63 * GR)]
    pltpu.make_async_copy(others, others, tile_send).wait()
    result.wait()


def gram_call(spin_bits, flip_energy, jacobian):
    vmem = pl.BlockSpec(memory_space=pltpu.VMEM)
    anywhere = pl.BlockSpec(memory_space=pl.ANY)
    return pl.pallas_call(
        gram_kernel,
        out_shape=(
            jax.ShapeDtypeStruct((PACKED, NB), jnp.float32),
            jax.ShapeDtypeStruct((GR, NB), jnp.float32),
            jax.ShapeDtypeStruct((N, WIDTH), jnp.bfloat16),
        ),
        in_specs=[vmem, vmem, anywhere],
        out_specs=(anywhere, vmem, anywhere),
        scratch_shapes=[
            pltpu.VMEM((N, WIDTH), jnp.bfloat16),
            pltpu.VMEM((PACKED, NB), jnp.float32),
            pltpu.VMEM((PACKED, NB), jnp.float32),
            pltpu.VMEM((64 * GR, NB), jnp.float32),
            pltpu.VMEM((2, ROWS_CORE, NB), jnp.float32),
            pltpu.VMEM((2, 4, ROWS_ONE, NB), jnp.float32),
            pltpu.VMEM((2, 4, ROWS_TWO, NB), jnp.float32),
            pltpu.VMEM((2, 8, 2 * ROWS_LAST, NB), jnp.float32),
            pltpu.VMEM((2, 8, 2 * ROWS_LAST, NB), jnp.float32),
            pltpu.SemaphoreType.DMA,
            pltpu.SemaphoreType.DMA((PIECES,)),
            pltpu.SemaphoreType.DMA,
            pltpu.SemaphoreType.DMA,
            pltpu.SemaphoreType.DMA,
            pltpu.SemaphoreType.DMA((PIECES,)),
            pltpu.SemaphoreType.DMA((2 * STEPS,)),
            pltpu.SemaphoreType.DMA((2 * STEPS,)),
        ],
        compiler_params=pltpu.CompilerParams(
            collective_id=0, has_side_effects=True, vmem_limit_bytes=48 * 1024 * 1024
        ),
        name="gram",
    )(spin_bits, flip_energy.reshape(1, PER), jacobian)


def split3(x):
    high = x.astype(jnp.bfloat16)
    rest = x - high.astype(jnp.float32)
    mid = rest.astype(jnp.bfloat16)
    low = (rest - mid.astype(jnp.float32)).astype(jnp.bfloat16)
    return high, mid, low


def dot_wide(a, b, turned=False):
    ah, am, al = split3(a)
    bh, bm, bl = split3(b)
    left = jnp.concatenate([ah, ah, am, am, ah, al], axis=1)
    right = jnp.concatenate([bh, bm, bh, bm, bl, bh], axis=1 if turned else 0)
    dims = (((1,), (1 if turned else 0,)), ((), ()))
    return lax.dot_general(left, right, dims, preferred_element_type=jnp.float32)


def lanes(v, c):
    return jnp.broadcast_to(v[:, c:c + 1], (GR, NB))


def subs(v, r):
    return jnp.broadcast_to(v[r:r + 1, :], (GR, NB))


def add_all(terms):
    while len(terms) > 1:
        terms = [terms[i] + terms[i + 1] for i in range(0, len(terms), 2)]
    return terms[0]


def invert_block(rows):
    lane = lax.broadcasted_iota(jnp.int32, (GR, NB), 1)
    sub = lax.broadcasted_iota(jnp.int32, (GR, NB), 0)
    count = NB // GR
    width = count // 2
    for low in range(0, count, width):
        high = low + width
        piv = [lanes(rows[low], low * GR + c) for c in range(GR)]
        for g in range(low, high):
            base = g * GR
            own = rows[g]
            more = g + 1 < high
            ahead = []
            if more:
                ahead = [lanes(own, base + GR + c) for c in range(GR)]
                coef_next = [lanes(rows[g + 1], base + q) for q in range(GR)]
                piv_next = [lanes(rows[g + 1], base + GR + c) for c in range(GR)]
            in_piv = (lane >= base) & (lane < base + GR)
            row = jnp.where(in_piv, jnp.where(lane - base == sub, 1.0, 0.0), own)
            for q in range(GR):
                at = sub == q
                inv = 1.0 / subs(piv[q], q)
                signed = jnp.where(at, -1.0, piv[q])
                coef = signed * inv
                if q + 1 < GR:
                    piv[q + 1] = jnp.where(at, 0.0, piv[q + 1]) - (signed * subs(piv[q + 1], q)) * inv
                for c in range(q + 2, GR):
                    piv[c] = jnp.where(at, 0.0, piv[c]) - coef * subs(piv[c], q)
                row = jnp.where(at, 0.0, row) - coef * subs(row, q)
                ahead = [jnp.where(at, 0.0, a) - coef * subs(a, q) for a in ahead]
            spread = [subs(row, q) for q in range(GR)]
            if more:
                piv = [
                    piv_next[c] - add_all([coef_next[q] * subs(ahead[c], q) for q in range(GR)]) for c in range(GR)
                ]
            new_rows = list(rows)
            new_rows[g] = row
            for v in range(low, high):
                if v == g:
                    continue
                coefs = coef_next if more and v == g + 1 else [lanes(rows[v], base + q) for q in range(GR)]
                new_rows[v] = jnp.where(in_piv, 0.0, rows[v]) - add_all([coefs[q] * spread[q] for q in range(GR)])
            rows = new_rows
        whole = jnp.concatenate(rows, axis=0)
        rest = jnp.concatenate(rows[:low] + rows[high:], axis=0)
        wide_lane = lax.broadcasted_iota(jnp.int32, rest.shape, 1)
        inside = (wide_lane >= low * GR) & (wide_lane < high * GR)
        rest = jnp.where(inside, 0.0, rest) - dot_wide(jnp.where(inside, rest, 0.0), whole)
        parts = [rest[i * GR:(i + 1) * GR, :] for i in range(count - width)]
        rows = parts[:low] + rows[low:high] + parts[low:]
    return rows


def solve_kernel(gram_ref, energy_ref, centred_ref, out_ref, work, held, x_row, x_col, sem):
    fetch = pltpu.make_async_copy(centred_ref, held, sem)
    fetch.start()
    sub = lax.broadcasted_iota(jnp.int32, (NB, NB), 0)
    lane = lax.broadcasted_iota(jnp.int32, (NB, NB), 1)
    eye = jnp.where(sub == lane, 1.0, 0.0)
    for i in range(BLOCKS):
        at = slice(i * NB, (i + 1) * NB)
        for j in range(i):
            work[at, j * NB:(j + 1) * NB] = gram_ref[block_at(i, j), :]
        work[at, at] = gram_ref[block_at(i, i), :] + 0.5 * eye
    tile = energy_ref[...]
    mean = jnp.sum(jnp.sum(tile, axis=1, keepdims=True), axis=0, keepdims=True) * (1.0 / N)
    tile = tile - mean
    for i in range(BLOCKS):
        work[N:N + GR, i * NB:(i + 1) * NB] = subs(tile, i)

    def stage(k, carry):
        at = pl.ds(pl.multiple_of(k * NB, NB), NB)
        rows = [work[pl.ds(pl.multiple_of(k * NB + v * GR, GR), GR), at] for v in range(NB // GR)]
        rows = invert_block(rows)
        for v in range(NB // GR):
            work[pl.ds(pl.multiple_of(k * NB + v * GR, GR), GR), at] = rows[v]
        for c in range(BLOCKS - 1):
            @pl.when(k == c)
            def _():
                own = slice(c * NB, (c + 1) * NB)
                after = slice((c + 1) * NB, N)
                below = slice((c + 1) * NB, N + GR)
                turned = dot_wide(work[own, own], work[after, own], turned=True)
                work[below, after] = work[below, after] - dot_wide(work[below, own], turned)
                work[own, after] = turned
        return carry

    lax.fori_loop(0, BLOCKS, stage, 0)

    for k in range(BLOCKS - 1, -1, -1):
        own = slice(k * NB, (k + 1) * NB)
        total = work[own, own] * work[N:N + 1, own]
        for j in range(k + 1, BLOCKS):
            col = slice(j * NB, (j + 1) * NB)
            total = total - work[own, col] * x_row[0:1, col]
        column = jnp.sum(total, axis=1, keepdims=True)
        column = jnp.broadcast_to(column, (NB, NB))
        x_row[0:1, own] = jnp.sum(column * eye, axis=0, keepdims=True)
        x_col[own, :] = column.astype(jnp.bfloat16).astype(jnp.float32)

    wide = x_row[0:1, :].astype(jnp.bfloat16).astype(jnp.float32)

    acc = jnp.zeros((NB, NB), jnp.float32)
    for i in range(BLOCKS):
        part = gram_ref[block_at(i, i), :] * (0.5 * wide[:, i * NB:(i + 1) * NB])
        for j in range(i):
            part = part + gram_ref[block_at(i, j), :] * wide[:, j * NB:(j + 1) * NB]
        acc = acc + part * x_col[i * NB:(i + 1) * NB, :]
    square_sum = 2.0 * jnp.sum(jnp.sum(acc, axis=0, keepdims=True), axis=1, keepdims=True)
    root_mean = jnp.sqrt(jnp.maximum(square_sum, 0.0) / PARAMS + 1e-06)
    fetch.wait()
    left = jnp.where(lax.broadcasted_iota(jnp.int32, (PER, N), 0) == 0, wide, 0.0).astype(jnp.bfloat16)
    direction = jnp.dot(left, held[...], preferred_element_type=jnp.float32)
    out_ref[...] = -direction[0:1, :] / root_mean


def solve_call(gram, energy, centred):
    vmem = pl.BlockSpec(memory_space=pltpu.VMEM)
    return pl.pallas_call(
        solve_kernel,
        out_shape=jax.ShapeDtypeStruct((1, WIDTH), jnp.float32),
        in_specs=[vmem, vmem, pl.BlockSpec(memory_space=pl.ANY)],
        out_specs=vmem,
        scratch_shapes=[
            pltpu.VMEM((N + GR, N), jnp.float32),
            pltpu.VMEM((N, WIDTH), jnp.bfloat16),
            pltpu.VMEM((GR, N), jnp.float32),
            pltpu.VMEM((N, NB), jnp.float32),
            pltpu.SemaphoreType.DMA,
        ],
        compiler_params=pltpu.CompilerParams(vmem_limit_bytes=48 * 1024 * 1024),
        name="solve",
    )(gram, energy, centred)


def on_device(spin_bits, flip_energy, jacobian):
    gram, energy, centred = gram_call(spin_bits, flip_energy, jacobian)
    return solve_call(gram, energy, centred).reshape(1, 1, -1)


def solution(mesh):
    return jax.shard_map(
        on_device,
        mesh=mesh,
        in_specs=(P("samp", None), P("samp"), P("samp", "par")),
        out_specs=P("par", "samp", None),
        check_vma=False,
    )
```

```python
import math

import jax
import jax.numpy as jnp
from jax import lax
from jax.experimental import pallas as pl
from jax.experimental.pallas import tpu as pltpu
from jax.sharding import PartitionSpec as P

SITES = 100
N = 1024
NB = 128
GR = 8
BLOCKS = N // NB
PARAMS = 786432
PER = 16
WIDTH = 3072
PIECES = 4
PIECE = WIDTH // PIECES
PACKED = BLOCKS * (BLOCKS + 1) // 2 * NB
HALF = PACKED // 2
ROWS_CORE = HALF // 2
ROWS_ONE = ROWS_CORE // 4
ROWS_TWO = ROWS_ONE // 4
ROWS_LAST = 8
STEPS = 8
MESH = pl.DeviceIdType.MESH


def block_at(i, j):
    start = (j * BLOCKS - j * (j - 1) // 2 + i - j) * NB
    return slice(start, start + NB)


def bond_weights():
    side = math.isqrt(SITES)
    site = lax.broadcasted_iota(jnp.int32, (SITES, SITES), 0)
    other = lax.broadcasted_iota(jnp.int32, (SITES, SITES), 1)
    row = (site * 205) >> 11
    col = site - row * side

    def bond(down, right):
        to_row, to_col = row + down, col + right
        to_row = jnp.where(to_row >= side, to_row - side, to_row)
        to_col = jnp.where(to_col >= side, to_col - side, jnp.where(to_col < 0, to_col + side, to_col))
        return jnp.where(other == to_row * side + to_col, 1.0, 0.0)

    return 0.25 * (bond(0, 1) + bond(1, 0)) + 0.125 * (bond(1, 1) + bond(1, -1))


def sum_blocks(place, device, packed, final, slots, sum_send, sum_recv):
    x, y, z, core = place
    slot_core, slot_one, slot_two, slot_last, staged = slots
    pos_one = x + core * (y - x)
    pos_two = y + core * (x - y)
    other_core = device(x, y, z, 1 - core)

    def on_one(at):
        return device(at + core * (x - at), y + core * (at - y), z, core)

    def on_two(at):
        return device(x + core * (at - x), at + core * (y - at), z, core)

    def rows(start, size):
        return pl.ds(pl.multiple_of(start, GR), size)

    def send(part, step, source, target, to):
        at = part * STEPS + step
        pltpu.make_async_remote_copy(
            src_ref=source, dst_ref=target, send_sem=sum_send.at[at], recv_sem=sum_recv.at[at],
            device_id=to, device_id_type=MESH,
        ).start()

    def likes(part):
        return (
            slot_core.at[part],
            slot_one.at[part, pl.ds(0, 3)],
            slot_two.at[part, pl.ds(0, 3)],
            slot_last.at[part, pl.ds(0, 7)],
            final.at[pl.ds(0, 7 * ROWS_LAST)],
            final.at[pl.ds(0, 3 * ROWS_TWO)],
            final.at[pl.ds(0, 3 * ROWS_ONE)],
            final.at[pl.ds(0, ROWS_CORE)],
        )

    def arrived(part, step):
        like = likes(part)[step]
        pltpu.make_async_copy(like, like, sum_recv.at[part * STEPS + step]).wait()

    def starts(part):
        half = part * HALF + core * ROWS_CORE
        one = half + pos_one * ROWS_ONE
        return half, one, one + pos_two * ROWS_TWO

    def to_core(part):
        source = packed.at[rows(part * HALF + (1 - core) * ROWS_CORE, ROWS_CORE)]
        send(part, 0, source, slot_core.at[part], other_core)

    def to_one(part):
        half, one, two = starts(part)
        arrived(part, 0)
        packed[rows(half, ROWS_CORE), :] = packed[rows(half, ROWS_CORE), :] + slot_core[part]
        for step in (2, 1, 3):
            to = (pos_one + step) % 4
            send(part, 1, packed.at[rows(half + to * ROWS_ONE, ROWS_ONE)], slot_one.at[part, pos_one], on_one(to))

    def add_three(start, size, slot, part, pos):
        at = rows(start, size)
        packed[at, :] = (packed[at, :] + slot[part, (pos + 1) % 4]) + (
            slot[part, (pos + 2) % 4] + slot[part, (pos + 3) % 4]
        )

    def to_two(part):
        half, one, two = starts(part)
        arrived(part, 1)
        add_three(one, ROWS_ONE, slot_one, part, pos_one)
        for step in (2, 1, 3):
            to = (pos_two + step) % 4
            send(part, 2, packed.at[rows(one + to * ROWS_TWO, ROWS_TWO)], slot_two.at[part, pos_two], on_two(to))

    def to_last(part):
        half, one, two = starts(part)
        arrived(part, 2)
        add_three(two, ROWS_TWO, slot_two, part, pos_two)
        spare = packed[rows(two + 8 * ROWS_LAST, ROWS_LAST), :]
        for i in range(8):
            staged[part, i, 0:ROWS_LAST] = packed[rows(two + i * ROWS_LAST, ROWS_LAST), :]
            staged[part, i, ROWS_LAST:2 * ROWS_LAST] = spare
        for step in (4, 3, 5, 2, 6, 1, 7):
            to = (z + step) % 8
            send(part, 3, staged.at[part, to], slot_last.at[part, z], device(x, y, to, core))

    def back_last(part):
        half, one, two = starts(part)
        slot_last[part, z] = staged[part, z]
        arrived(part, 3)
        total = slot_last[part, 0]
        for i in range(1, 8):
            total = total + slot_last[part, i]
        last = rows(two + z * ROWS_LAST, ROWS_LAST)
        final[last, :] = total[0:ROWS_LAST]
        final[rows(two + 8 * ROWS_LAST, ROWS_LAST), :] = total[ROWS_LAST:2 * ROWS_LAST]
        for step in (4, 3, 5, 2, 6, 1, 7):
            send(part, 4, final.at[last], final.at[last], device(x, y, (z + step) % 8, core))

    def back_two(part):
        half, one, two = starts(part)
        arrived(part, 4)
        for step in (2, 1, 3):
            own = final.at[rows(two, ROWS_TWO)]
            send(part, 5, own, own, on_two((pos_two + step) % 4))

    def back_one(part):
        half, one, two = starts(part)
        arrived(part, 5)
        for step in (2, 1, 3):
            own = final.at[rows(one, ROWS_ONE)]
            send(part, 6, own, own, on_one((pos_one + step) % 4))

    def back_core(part):
        half, one, two = starts(part)
        arrived(part, 6)
        own = final.at[rows(half, ROWS_CORE)]
        send(part, 7, own, own, other_core)

    moves = (to_core, to_one, to_two, to_last, back_last, back_two, back_one, back_core)

    def first_half():
        for at in range(STEPS):
            moves[at](0)
            if at:
                moves[at - 1](1)
        arrived(0, STEPS - 1)

    def second_half():
        moves[STEPS - 1](1)
        arrived(1, STEPS - 1)

    def finish():
        for part in range(2):
            for step in range(STEPS):
                like = likes(part)[step]
                pltpu.make_async_copy(like, like, sum_send.at[part * STEPS + step]).wait()

    return first_half, second_half, finish


def split3(x):
    high = x.astype(jnp.bfloat16)
    rest = x - high.astype(jnp.float32)
    mid = rest.astype(jnp.bfloat16)
    low = (rest - mid.astype(jnp.float32)).astype(jnp.bfloat16)
    return high, mid, low


def dot_wide(a, b, turned=False):
    ah, am, al = split3(a)
    bh, bm, bl = split3(b)
    left = jnp.concatenate([ah, ah, am, am, ah, al], axis=1)
    right = jnp.concatenate([bh, bm, bh, bm, bl, bh], axis=1 if turned else 0)
    dims = (((1,), (1 if turned else 0,)), ((), ()))
    return lax.dot_general(left, right, dims, preferred_element_type=jnp.float32)


def lanes(v, c):
    return jnp.broadcast_to(v[:, c:c + 1], (GR, NB))


def subs(v, r):
    return jnp.broadcast_to(v[r:r + 1, :], (GR, NB))


def add_all(terms):
    while len(terms) > 1:
        terms = [terms[i] + terms[i + 1] for i in range(0, len(terms), 2)]
    return terms[0]


def invert_block(rows):
    lane = lax.broadcasted_iota(jnp.int32, (GR, NB), 1)
    sub = lax.broadcasted_iota(jnp.int32, (GR, NB), 0)
    count = NB // GR
    width = count // 2
    for low in range(0, count, width):
        high = low + width
        piv = [lanes(rows[low], low * GR + c) for c in range(GR)]
        for g in range(low, high):
            base = g * GR
            own = rows[g]
            more = g + 1 < high
            ahead = []
            if more:
                ahead = [lanes(own, base + GR + c) for c in range(GR)]
                coef_next = [lanes(rows[g + 1], base + q) for q in range(GR)]
                piv_next = [lanes(rows[g + 1], base + GR + c) for c in range(GR)]
            in_piv = (lane >= base) & (lane < base + GR)
            row = jnp.where(in_piv, jnp.where(lane - base == sub, 1.0, 0.0), own)
            for q in range(GR):
                at = sub == q
                inv = 1.0 / subs(piv[q], q)
                signed = jnp.where(at, -1.0, piv[q])
                coef = signed * inv
                if q + 1 < GR:
                    piv[q + 1] = jnp.where(at, 0.0, piv[q + 1]) - (signed * subs(piv[q + 1], q)) * inv
                for c in range(q + 2, GR):
                    piv[c] = jnp.where(at, 0.0, piv[c]) - coef * subs(piv[c], q)
                row = jnp.where(at, 0.0, row) - coef * subs(row, q)
                ahead = [jnp.where(at, 0.0, a) - coef * subs(a, q) for a in ahead]
            spread = [subs(row, q) for q in range(GR)]
            if more:
                piv = [
                    piv_next[c] - add_all([coef_next[q] * subs(ahead[c], q) for q in range(GR)]) for c in range(GR)
                ]
            new_rows = list(rows)
            new_rows[g] = row
            for v in range(low, high):
                if v == g:
                    continue
                coefs = coef_next if more and v == g + 1 else [lanes(rows[v], base + q) for q in range(GR)]
                new_rows[v] = jnp.where(in_piv, 0.0, rows[v]) - add_all([coefs[q] * spread[q] for q in range(GR)])
            rows = new_rows
        whole = jnp.concatenate(rows, axis=0)
        rest = jnp.concatenate(rows[:low] + rows[high:], axis=0)
        wide_lane = lax.broadcasted_iota(jnp.int32, rest.shape, 1)
        inside = (wide_lane >= low * GR) & (wide_lane < high * GR)
        rest = jnp.where(inside, 0.0, rest) - dot_wide(jnp.where(inside, rest, 0.0), whole)
        parts = [rest[i * GR:(i + 1) * GR, :] for i in range(count - width)]
        rows = parts[:low] + rows[low:high] + parts[low:]
    return rows


def solve(energy, second_half, final, held, work, x_row, x_col):
    sub = lax.broadcasted_iota(jnp.int32, (NB, NB), 0)
    lane = lax.broadcasted_iota(jnp.int32, (NB, NB), 1)
    eye = jnp.where(sub == lane, 1.0, 0.0)

    def unpack(part):
        blocks = [(i, j) for j in range(BLOCKS) for i in range(j, BLOCKS)]
        for i, j in blocks[part * len(blocks) // 2:(part + 1) * len(blocks) // 2]:
            block = final[block_at(i, j), :]
            work[i * NB:(i + 1) * NB, j * NB:(j + 1) * NB] = block + 0.5 * eye if i == j else block

    unpack(0)
    tile = energy
    mean = jnp.sum(jnp.sum(tile, axis=1, keepdims=True), axis=0, keepdims=True) * (1.0 / N)
    tile = tile - mean
    for i in range(BLOCKS):
        work[N:N + GR, i * NB:(i + 1) * NB] = subs(tile, i)

    def stage(k, carry):
        at = pl.ds(pl.multiple_of(k * NB, NB), NB)
        rows = [work[pl.ds(pl.multiple_of(k * NB + v * GR, GR), GR), at] for v in range(NB // GR)]
        rows = invert_block(rows)
        for v in range(NB // GR):
            work[pl.ds(pl.multiple_of(k * NB + v * GR, GR), GR), at] = rows[v]

        @pl.when(k == 0)
        def _():
            second_half()
            unpack(1)

        for c in range(BLOCKS - 1):
            @pl.when(k == c)
            def _():
                own = slice(c * NB, (c + 1) * NB)
                after = slice((c + 1) * NB, N)
                below = slice((c + 1) * NB, N + GR)
                turned = dot_wide(work[own, own], work[after, own], turned=True)
                work[below, after] = work[below, after] - dot_wide(work[below, own], turned)
                work[own, after] = turned
        return carry

    lax.fori_loop(0, BLOCKS, stage, 0)

    for k in range(BLOCKS - 1, -1, -1):
        own = slice(k * NB, (k + 1) * NB)
        total = work[own, own] * work[N:N + 1, own]
        for j in range(k + 1, BLOCKS):
            col = slice(j * NB, (j + 1) * NB)
            total = total - work[own, col] * x_row[0:1, col]
        column = jnp.sum(total, axis=1, keepdims=True)
        column = jnp.broadcast_to(column, (NB, NB))
        x_row[0:1, own] = jnp.sum(column * eye, axis=0, keepdims=True)
        x_col[own, :] = column.astype(jnp.bfloat16).astype(jnp.float32)

    wide = x_row[0:1, :].astype(jnp.bfloat16).astype(jnp.float32)

    acc = jnp.zeros((NB, NB), jnp.float32)
    for i in range(BLOCKS):
        part = final[block_at(i, i), :] * (0.5 * wide[:, i * NB:(i + 1) * NB])
        for j in range(i):
            part = part + final[block_at(i, j), :] * wide[:, j * NB:(j + 1) * NB]
        acc = acc + part * x_col[i * NB:(i + 1) * NB, :]
    square_sum = 2.0 * jnp.sum(jnp.sum(acc, axis=0, keepdims=True), axis=1, keepdims=True)
    root_mean = jnp.sqrt(jnp.maximum(square_sum, 0.0) / PARAMS + 1e-06)
    left = jnp.where(lax.broadcasted_iota(jnp.int32, (PER, N), 0) == 0, wide, 0.0).astype(jnp.bfloat16)
    direction = jnp.dot(left, held[...], preferred_element_type=jnp.float32)
    return -direction[0:1, :] / root_mean


def update_kernel(
    spin_any, flip_any, jac_ref, out_ref,
    spin_ref, flip_ref, held, packed, final, tiles, slot_core, slot_one, slot_two, slot_last, staged, work, x_row, x_col,
    send_sem, recv_sem, own_sem, spin_sem, flip_sem, tile_send, tile_recv, sum_send, sum_recv,
):
    samp, par = lax.axis_index("samp"), lax.axis_index("par")
    core = par % 2
    x_hi, y, z = samp // 32, (samp // 8) % 4, samp % 8
    x = x_hi * 2 + par // 2

    def device(x_at, y_at, z_at, core_at):
        return {"samp": (x_at // 2) * 32 + y_at * 8 + z_at, "par": (x_at % 2) * 2 + core_at}

    spins = pltpu.make_async_copy(spin_any, spin_ref, spin_sem)
    spins.start()
    flips = pltpu.make_async_copy(flip_any, flip_ref, flip_sem)
    flips.start()
    barrier = pltpu.get_barrier_semaphore()

    def greet(step, carry):
        pl.semaphore_signal(
            barrier, inc=1, device_id={"samp": lax.rem(samp + step, 64), "par": par}, device_id_type=MESH
        )
        return carry

    lax.fori_loop(1, 64, greet, 0)
    for partner in (device(x, y, z, 1 - core), device((x + 1) % 4, y, z, core), device((x + 3) % 4, y, z, core)):
        pl.semaphore_signal(barrier, inc=1, device_id=partner, device_id_type=MESH)

    mine = pl.ds(pl.multiple_of(samp * PER, PER), PER)
    own = pltpu.make_async_copy(
        jac_ref.at[:, pl.ds(pl.multiple_of(samp * WIDTH, NB), WIDTH)], held.at[mine], own_sem
    )
    own.start()
    packed[...] = jnp.zeros_like(packed)
    spins.wait()
    flips.wait()

    signs = (2 * spin_ref[...] - 1).astype(jnp.float32).astype(jnp.bfloat16)
    linked = jnp.dot(signs, bond_weights().astype(jnp.bfloat16), preferred_element_type=jnp.float32)
    bonds = jnp.sum(linked * signs.astype(jnp.float32), axis=1, keepdims=True)
    square = (PER, PER)
    same = lax.broadcasted_iota(jnp.int32, square, 0) == lax.broadcasted_iota(jnp.int32, square, 1)
    values = bonds + jnp.sum(jnp.where(same, flip_ref[...], 0.0), axis=1, keepdims=True)
    lane = lax.broadcasted_iota(jnp.int32, (PER, NB), 1)
    sample = lax.broadcasted_iota(jnp.int32, (PER, NB), 0)
    line = jnp.sum(jnp.where(lane == sample + (samp % 8) * PER, values, 0.0), axis=0, keepdims=True)
    sub = lax.broadcasted_iota(jnp.int32, (GR, NB), 0)
    tile_at = pl.ds(pl.multiple_of(samp * GR, GR), GR)
    tiles[tile_at, :] = jnp.where(sub == samp // 8, line, 0.0)

    pl.semaphore_wait(barrier, 66)

    def send_tile(step, carry):
        pltpu.make_async_remote_copy(
            src_ref=tiles.at[tile_at],
            dst_ref=tiles.at[tile_at],
            send_sem=tile_send,
            recv_sem=tile_recv,
            device_id={"samp": lax.rem(samp + step, 64), "par": par},
            device_id_type=MESH,
        ).start()
        return carry

    def send_block(piece, x_to, y_to, z_to):
        to = x_to * 32 + y_to * 8 + z_to
        pltpu.make_async_remote_copy(
            src_ref=jac_ref.at[:, pl.ds(pl.multiple_of(to * WIDTH + piece * PIECE, NB), PIECE)],
            dst_ref=held.at[mine, pl.ds(pl.multiple_of(piece * PIECE, NB), PIECE)],
            send_sem=send_sem,
            recv_sem=recv_sem.at[piece],
            device_id={"samp": to, "par": par},
            device_id_type=MESH,
        ).start()

    def send_plane(step, carry):
        piece, plane = step // 8, step % 8
        x_to = (x_hi + 1 - plane // 4) % 2
        y_to = (y + 6 - plane % 4) % 4
        for z_off in (4, 7, 3, 5, 2, 6, 1):
            send_block(piece, x_to, y_to, (z + z_off) % 8)

        @pl.when(plane != 6)
        def _():
            send_block(piece, x_to, y_to, z)

        return carry

    lax.fori_loop(0, 8 * PIECES, send_plane, 0)
    lax.fori_loop(1, 64, send_tile, 0)
    own.wait()

    def work_piece(piece, carry):
        cols = pl.ds(pl.multiple_of(piece * PIECE, NB), PIECE)
        others = held.at[pl.ds(0, N - PER), cols]
        pltpu.make_async_copy(others, others, recv_sem.at[piece]).wait()

        def add_rows(i, total):
            return total + held[pl.ds(pl.multiple_of(i * PER, PER), PER), cols].astype(jnp.float32)

        total = lax.fori_loop(0, N // PER, add_rows, jnp.zeros((PER, PIECE), jnp.float32), unroll=4)
        mean = jnp.sum(total, axis=0, keepdims=True) * (1.0 / N)

        def centre_rows(i, carry):
            at = pl.ds(pl.multiple_of(i * PER, PER), PER)
            held[at, cols] = (held[at, cols].astype(jnp.float32) - mean).astype(jnp.bfloat16)
            return carry

        lax.fori_loop(0, N // PER, centre_rows, 0, unroll=4)
        for i in range(0, BLOCKS, 2):
            size = (i + 2) * NB
            product = lax.dot_general(
                held[i * NB:size, cols], held[0:size, cols], (((1,), (1,)), ((), ())),
                preferred_element_type=jnp.float32,
            )
            for r in range(2):
                for j in range(i + r + 1):
                    at = block_at(i + r, j)
                    packed[at, :] = packed[at, :] + product[r * NB:(r + 1) * NB, j * NB:(j + 1) * NB]
        return carry

    lax.fori_loop(0, PIECES, work_piece, 0)

    slots = (slot_core, slot_one, slot_two, slot_last, staged)
    first_half, second_half, finish = sum_blocks((x, y, z, core), device, packed, final, slots, sum_send, sum_recv)
    first_half()

    others = tiles.at[pl.ds(0, 63 * GR)]
    pltpu.make_async_copy(others, others, tile_recv).wait()
    energy = tiles[0:GR, :]
    for i in range(1, 64):
        energy = energy + tiles[i * GR:(i + 1) * GR, :]

    direction = solve(energy, second_half, final, held, work, x_row, x_col)
    out_ref[...] = direction

    others = held.at[pl.ds(0, N - PER)]
    pltpu.make_async_copy(others, others, send_sem).wait()
    others = tiles.at[pl.ds(0, 63 * GR)]
    pltpu.make_async_copy(others, others, tile_send).wait()
    finish()


def update_call(spin_bits, flip_energy, jacobian):
    anywhere = pl.BlockSpec(memory_space=pl.ANY)
    return pl.pallas_call(
        update_kernel,
        out_shape=jax.ShapeDtypeStruct((1, WIDTH), jnp.float32),
        in_specs=[anywhere, anywhere, anywhere],
        out_specs=pl.BlockSpec(memory_space=pltpu.VMEM),
        scratch_shapes=[
            pltpu.VMEM((PER, SITES), jnp.int32),
            pltpu.VMEM((1, PER), jnp.float32),
            pltpu.VMEM((N, WIDTH), jnp.bfloat16),
            pltpu.VMEM((PACKED, NB), jnp.float32),
            pltpu.VMEM((PACKED, NB), jnp.float32),
            pltpu.VMEM((64 * GR, NB), jnp.float32),
            pltpu.VMEM((2, ROWS_CORE, NB), jnp.float32),
            pltpu.VMEM((2, 4, ROWS_ONE, NB), jnp.float32),
            pltpu.VMEM((2, 4, ROWS_TWO, NB), jnp.float32),
            pltpu.VMEM((2, 8, 2 * ROWS_LAST, NB), jnp.float32),
            pltpu.VMEM((2, 8, 2 * ROWS_LAST, NB), jnp.float32),
            pltpu.VMEM((N + GR, N), jnp.float32),
            pltpu.VMEM((GR, N), jnp.float32),
            pltpu.VMEM((N, NB), jnp.float32),
            pltpu.SemaphoreType.DMA,
            pltpu.SemaphoreType.DMA((PIECES,)),
            pltpu.SemaphoreType.DMA,
            pltpu.SemaphoreType.DMA,
            pltpu.SemaphoreType.DMA,
            pltpu.SemaphoreType.DMA,
            pltpu.SemaphoreType.DMA,
            pltpu.SemaphoreType.DMA((2 * STEPS,)),
            pltpu.SemaphoreType.DMA((2 * STEPS,)),
        ],
        compiler_params=pltpu.CompilerParams(
            collective_id=0, has_side_effects=True, vmem_limit_bytes=60 * 1024 * 1024
        ),
        name="update",
    )(spin_bits, flip_energy.reshape(1, PER), jacobian)


def on_device(spin_bits, flip_energy, jacobian):
    return update_call(spin_bits, flip_energy, jacobian).reshape(1, 1, -1)


def solution(mesh):
    return jax.shard_map(
        on_device,
        mesh=mesh,
        in_specs=(P("samp", None), P("samp"), P("samp", "par")),
        out_specs=P("par", "samp", None),
        check_vma=False,
    )
```

```python
import math

import jax
import jax.numpy as jnp
from jax import lax
from jax.experimental import pallas as pl
from jax.experimental.pallas import tpu as pltpu
from jax.sharding import PartitionSpec as P

SITES = 100
N = 1024
NB = 128
GR = 8
BLOCKS = N // NB
PARAMS = 786432
PER = 16
WIDTH = 3072
PIECES = 4
PIECE = WIDTH // PIECES
PACKED = BLOCKS * (BLOCKS + 1) // 2 * NB
HALF = PACKED // 2
ROWS_CORE = HALF // 2
ROWS_ONE = ROWS_CORE // 4
ROWS_TWO = ROWS_ONE // 4
ROWS_LAST = 8
STEPS = 8
MESH = pl.DeviceIdType.MESH


def block_at(i, j):
    start = (j * BLOCKS - j * (j - 1) // 2 + i - j) * NB
    return slice(start, start + NB)


def bond_weights():
    side = math.isqrt(SITES)
    site = lax.broadcasted_iota(jnp.int32, (SITES, SITES), 0)
    other = lax.broadcasted_iota(jnp.int32, (SITES, SITES), 1)
    row = (site * 205) >> 11
    col = site - row * side

    def bond(down, right):
        to_row, to_col = row + down, col + right
        to_row = jnp.where(to_row >= side, to_row - side, to_row)
        to_col = jnp.where(to_col >= side, to_col - side, jnp.where(to_col < 0, to_col + side, to_col))
        return jnp.where(other == to_row * side + to_col, 1.0, 0.0)

    return 0.25 * (bond(0, 1) + bond(1, 0)) + 0.125 * (bond(1, 1) + bond(1, -1))


def sum_blocks(place, device, packed, final, slots, sum_send, sum_recv):
    x, y, z, core = place
    slot_core, slot_one, slot_two, slot_last, staged = slots
    pos_one = x + core * (y - x)
    pos_two = y + core * (x - y)
    other_core = device(x, y, z, 1 - core)

    def on_one(at):
        return device(at + core * (x - at), y + core * (at - y), z, core)

    def on_two(at):
        return device(x + core * (at - x), at + core * (y - at), z, core)

    def rows(start, size):
        return pl.ds(pl.multiple_of(start, GR), size)

    def send(part, step, source, target, to):
        at = part * STEPS + step
        pltpu.make_async_remote_copy(
            src_ref=source, dst_ref=target, send_sem=sum_send.at[at], recv_sem=sum_recv.at[at],
            device_id=to, device_id_type=MESH,
        ).start()

    def likes(part):
        return (
            slot_core.at[part],
            slot_one.at[part, pl.ds(0, 3)],
            slot_two.at[part, pl.ds(0, 3)],
            slot_last.at[part, pl.ds(0, 7)],
            final.at[pl.ds(0, 7 * ROWS_LAST)],
            final.at[pl.ds(0, 3 * ROWS_TWO)],
            final.at[pl.ds(0, 3 * ROWS_ONE)],
            final.at[pl.ds(0, ROWS_CORE)],
        )

    def arrived(part, step):
        like = likes(part)[step]
        pltpu.make_async_copy(like, like, sum_recv.at[part * STEPS + step]).wait()

    def starts(part):
        half = part * HALF + core * ROWS_CORE
        one = half + pos_one * ROWS_ONE
        return half, one, one + pos_two * ROWS_TWO

    def to_core(part):
        source = packed.at[rows(part * HALF + (1 - core) * ROWS_CORE, ROWS_CORE)]
        send(part, 0, source, slot_core.at[part], other_core)

    def to_one(part):
        half, one, two = starts(part)
        arrived(part, 0)
        packed[rows(half, ROWS_CORE), :] = packed[rows(half, ROWS_CORE), :] + slot_core[part]
        for step in (2, 1, 3):
            to = (pos_one + step) % 4
            send(part, 1, packed.at[rows(half + to * ROWS_ONE, ROWS_ONE)], slot_one.at[part, pos_one], on_one(to))

    def add_three(start, size, slot, part, pos):
        at = rows(start, size)
        packed[at, :] = (packed[at, :] + slot[part, (pos + 1) % 4]) + (
            slot[part, (pos + 2) % 4] + slot[part, (pos + 3) % 4]
        )

    def to_two(part):
        half, one, two = starts(part)
        arrived(part, 1)
        add_three(one, ROWS_ONE, slot_one, part, pos_one)
        for step in (2, 1, 3):
            to = (pos_two + step) % 4
            send(part, 2, packed.at[rows(one + to * ROWS_TWO, ROWS_TWO)], slot_two.at[part, pos_two], on_two(to))

    def to_last(part):
        half, one, two = starts(part)
        arrived(part, 2)
        add_three(two, ROWS_TWO, slot_two, part, pos_two)
        spare = packed[rows(two + 8 * ROWS_LAST, ROWS_LAST), :]
        for i in range(8):
            staged[part, i, 0:ROWS_LAST] = packed[rows(two + i * ROWS_LAST, ROWS_LAST), :]
            staged[part, i, ROWS_LAST:2 * ROWS_LAST] = spare
        for step in (4, 3, 5, 2, 6, 1, 7):
            to = (z + step) % 8
            send(part, 3, staged.at[part, to], slot_last.at[part, z], device(x, y, to, core))

    def back_last(part):
        half, one, two = starts(part)
        slot_last[part, z] = staged[part, z]
        arrived(part, 3)
        total = slot_last[part, 0]
        for i in range(1, 8):
            total = total + slot_last[part, i]
        last = rows(two + z * ROWS_LAST, ROWS_LAST)
        final[last, :] = total[0:ROWS_LAST]
        final[rows(two + 8 * ROWS_LAST, ROWS_LAST), :] = total[ROWS_LAST:2 * ROWS_LAST]
        for step in (4, 3, 5, 2, 6, 1, 7):
            send(part, 4, final.at[last], final.at[last], device(x, y, (z + step) % 8, core))

    def back_two(part):
        half, one, two = starts(part)
        arrived(part, 4)
        for step in (2, 1, 3):
            own = final.at[rows(two, ROWS_TWO)]
            send(part, 5, own, own, on_two((pos_two + step) % 4))

    def back_one(part):
        half, one, two = starts(part)
        arrived(part, 5)
        for step in (2, 1, 3):
            own = final.at[rows(one, ROWS_ONE)]
            send(part, 6, own, own, on_one((pos_one + step) % 4))

    def back_core(part):
        half, one, two = starts(part)
        arrived(part, 6)
        own = final.at[rows(half, ROWS_CORE)]
        send(part, 7, own, own, other_core)

    moves = (to_core, to_one, to_two, to_last, back_last, back_two, back_one, back_core)

    def first_half():
        for move in moves:
            for part in range(2):
                move(part)
        arrived(0, STEPS - 1)

    def second_half():
        arrived(1, STEPS - 1)

    def finish():
        for part in range(2):
            for step in range(STEPS):
                like = likes(part)[step]
                pltpu.make_async_copy(like, like, sum_send.at[part * STEPS + step]).wait()

    return first_half, second_half, finish


def split3(x):
    high = x.astype(jnp.bfloat16)
    rest = x - high.astype(jnp.float32)
    mid = rest.astype(jnp.bfloat16)
    low = (rest - mid.astype(jnp.float32)).astype(jnp.bfloat16)
    return high, mid, low


def dot_wide(a, b, turned=False):
    ah, am, al = split3(a)
    bh, bm, bl = split3(b)
    left = jnp.concatenate([ah, ah, am, am, ah, al], axis=1)
    right = jnp.concatenate([bh, bm, bh, bm, bl, bh], axis=1 if turned else 0)
    dims = (((1,), (1 if turned else 0,)), ((), ()))
    return lax.dot_general(left, right, dims, preferred_element_type=jnp.float32)


def lanes(v, c):
    return jnp.broadcast_to(v[:, c:c + 1], (GR, NB))


def subs(v, r):
    return jnp.broadcast_to(v[r:r + 1, :], (GR, NB))


def add_all(terms):
    while len(terms) > 1:
        terms = [terms[i] + terms[i + 1] for i in range(0, len(terms), 2)]
    return terms[0]


def invert_block(rows):
    lane = lax.broadcasted_iota(jnp.int32, (GR, NB), 1)
    sub = lax.broadcasted_iota(jnp.int32, (GR, NB), 0)
    count = NB // GR
    width = count // 2
    for low in range(0, count, width):
        high = low + width
        piv = [lanes(rows[low], low * GR + c) for c in range(GR)]
        for g in range(low, high):
            base = g * GR
            own = rows[g]
            more = g + 1 < high
            ahead = []
            if more:
                ahead = [lanes(own, base + GR + c) for c in range(GR)]
                coef_next = [lanes(rows[g + 1], base + q) for q in range(GR)]
                piv_next = [lanes(rows[g + 1], base + GR + c) for c in range(GR)]
            in_piv = (lane >= base) & (lane < base + GR)
            row = jnp.where(in_piv, jnp.where(lane - base == sub, 1.0, 0.0), own)
            for q in range(GR):
                at = sub == q
                inv = 1.0 / subs(piv[q], q)
                signed = jnp.where(at, -1.0, piv[q])
                coef = signed * inv
                if q + 1 < GR:
                    piv[q + 1] = jnp.where(at, 0.0, piv[q + 1]) - (signed * subs(piv[q + 1], q)) * inv
                for c in range(q + 2, GR):
                    piv[c] = jnp.where(at, 0.0, piv[c]) - coef * subs(piv[c], q)
                row = jnp.where(at, 0.0, row) - coef * subs(row, q)
                ahead = [jnp.where(at, 0.0, a) - coef * subs(a, q) for a in ahead]
            spread = [subs(row, q) for q in range(GR)]
            if more:
                piv = [
                    piv_next[c] - add_all([coef_next[q] * subs(ahead[c], q) for q in range(GR)]) for c in range(GR)
                ]
            new_rows = list(rows)
            new_rows[g] = row
            for v in [*range(g + 1, high), *range(low, g)]:
                coefs = coef_next if more and v == g + 1 else [lanes(rows[v], base + q) for q in range(GR)]
                new_rows[v] = jnp.where(in_piv, 0.0, rows[v]) - add_all([coefs[q] * spread[q] for q in range(GR)])
            rows = new_rows
        whole = jnp.concatenate(rows, axis=0)
        rest = jnp.concatenate(rows[:low] + rows[high:], axis=0)
        wide_lane = lax.broadcasted_iota(jnp.int32, rest.shape, 1)
        inside = (wide_lane >= low * GR) & (wide_lane < high * GR)
        rest = jnp.where(inside, 0.0, rest) - dot_wide(jnp.where(inside, rest, 0.0), whole)
        parts = [rest[i * GR:(i + 1) * GR, :] for i in range(count - width)]
        rows = parts[:low] + rows[low:high] + parts[low:]
    return rows


def solve(energy, second_half, final, held, work, x_row, x_col):
    sub = lax.broadcasted_iota(jnp.int32, (NB, NB), 0)
    lane = lax.broadcasted_iota(jnp.int32, (NB, NB), 1)
    eye = jnp.where(sub == lane, 1.0, 0.0)

    def unpack(part):
        blocks = [(i, j) for j in range(BLOCKS) for i in range(j, BLOCKS)]
        for i, j in blocks[part * len(blocks) // 2:(part + 1) * len(blocks) // 2]:
            block = final[block_at(i, j), :]
            work[i * NB:(i + 1) * NB, j * NB:(j + 1) * NB] = block + 0.5 * eye if i == j else block

    unpack(0)
    tile = energy
    mean = jnp.sum(jnp.sum(tile, axis=1, keepdims=True), axis=0, keepdims=True) * (1.0 / N)
    tile = tile - mean
    for i in range(BLOCKS):
        work[N:N + GR, i * NB:(i + 1) * NB] = subs(tile, i)

    def stage(k, carry):
        at = pl.ds(pl.multiple_of(k * NB, NB), NB)
        rows = [work[pl.ds(pl.multiple_of(k * NB + v * GR, GR), GR), at] for v in range(NB // GR)]
        rows = invert_block(rows)
        for v in range(NB // GR):
            work[pl.ds(pl.multiple_of(k * NB + v * GR, GR), GR), at] = rows[v]

        @pl.when(k == 0)
        def _():
            second_half()
            unpack(1)

        for c in range(BLOCKS - 1):
            @pl.when(k == c)
            def _():
                own = slice(c * NB, (c + 1) * NB)
                after = slice((c + 1) * NB, N)
                below = slice((c + 1) * NB, N + GR)
                turned = dot_wide(work[own, own], work[after, own], turned=True)
                work[below, after] = work[below, after] - dot_wide(work[below, own], turned)
                work[own, after] = turned
        return carry

    lax.fori_loop(0, BLOCKS, stage, 0)

    direction = jnp.zeros((PER, WIDTH), jnp.float32)
    for k in range(BLOCKS - 1, -1, -1):
        own = slice(k * NB, (k + 1) * NB)
        total = work[own, own] * work[N:N + 1, own]
        for j in range(k + 1, BLOCKS):
            col = slice(j * NB, (j + 1) * NB)
            total = total - work[own, col] * x_row[0:1, col]
        column = jnp.sum(total, axis=1, keepdims=True)
        column = jnp.broadcast_to(column, (NB, NB))
        x_row[0:1, own] = jnp.sum(column * eye, axis=0, keepdims=True)
        x_col[own, :] = column.astype(jnp.bfloat16).astype(jnp.float32)
        if k % 2 == 0:
            pair = slice(k * NB, (k + 2) * NB)
            weights = jnp.broadcast_to(x_row[0:1, pair], (PER, 2 * NB)).astype(jnp.bfloat16)
            direction = direction + jnp.dot(weights, held[pair, :], preferred_element_type=jnp.float32)

    wide = x_row[0:1, :].astype(jnp.bfloat16).astype(jnp.float32)

    acc = jnp.zeros((NB, NB), jnp.float32)
    for i in range(BLOCKS):
        part = final[block_at(i, i), :] * (0.5 * wide[:, i * NB:(i + 1) * NB])
        for j in range(i):
            part = part + final[block_at(i, j), :] * wide[:, j * NB:(j + 1) * NB]
        acc = acc + part * x_col[i * NB:(i + 1) * NB, :]
    square_sum = 2.0 * jnp.sum(jnp.sum(acc, axis=0, keepdims=True), axis=1, keepdims=True)
    root_mean = jnp.sqrt(jnp.maximum(square_sum, 0.0) / PARAMS + 1e-06)
    return -direction[0:1, :] / root_mean


def update_kernel(
    spin_any, flip_any, jac_ref, out_ref,
    spin_ref, flip_ref, held, packed, final, tiles, slot_core, slot_one, slot_two, slot_last, staged, work, x_row, x_col,
    send_sem, recv_sem, own_sem, spin_sem, flip_sem, tile_send, tile_recv, sum_send, sum_recv,
):
    samp, par = lax.axis_index("samp"), lax.axis_index("par")
    core = par % 2
    x_hi, y, z = samp // 32, (samp // 8) % 4, samp % 8
    x = x_hi * 2 + par // 2

    def device(x_at, y_at, z_at, core_at):
        return {"samp": (x_at // 2) * 32 + y_at * 8 + z_at, "par": (x_at % 2) * 2 + core_at}

    spins = pltpu.make_async_copy(spin_any, spin_ref, spin_sem)
    spins.start()
    flips = pltpu.make_async_copy(flip_any, flip_ref, flip_sem)
    flips.start()
    barrier = pltpu.get_barrier_semaphore()

    def greet(step, carry):
        pl.semaphore_signal(
            barrier, inc=1, device_id={"samp": lax.rem(samp + step, 64), "par": par}, device_id_type=MESH
        )
        return carry

    lax.fori_loop(1, 64, greet, 0)
    for partner in (device(x, y, z, 1 - core), device((x + 1) % 4, y, z, core), device((x + 3) % 4, y, z, core)):
        pl.semaphore_signal(barrier, inc=1, device_id=partner, device_id_type=MESH)

    mine = pl.ds(pl.multiple_of(samp * PER, PER), PER)
    own = pltpu.make_async_copy(
        jac_ref.at[:, pl.ds(pl.multiple_of(samp * WIDTH, NB), WIDTH)], held.at[mine], own_sem
    )
    own.start()
    packed[...] = jnp.zeros_like(packed)
    spins.wait()
    flips.wait()

    signs = (2 * spin_ref[...] - 1).astype(jnp.float32).astype(jnp.bfloat16)
    linked = jnp.dot(signs, bond_weights().astype(jnp.bfloat16), preferred_element_type=jnp.float32)
    bonds = jnp.sum(linked * signs.astype(jnp.float32), axis=1, keepdims=True)
    square = (PER, PER)
    same = lax.broadcasted_iota(jnp.int32, square, 0) == lax.broadcasted_iota(jnp.int32, square, 1)
    values = bonds + jnp.sum(jnp.where(same, flip_ref[...], 0.0), axis=1, keepdims=True)
    lane = lax.broadcasted_iota(jnp.int32, (PER, NB), 1)
    sample = lax.broadcasted_iota(jnp.int32, (PER, NB), 0)
    line = jnp.sum(jnp.where(lane == sample + (samp % 8) * PER, values, 0.0), axis=0, keepdims=True)
    sub = lax.broadcasted_iota(jnp.int32, (GR, NB), 0)
    tile_at = pl.ds(pl.multiple_of(samp * GR, GR), GR)
    tiles[tile_at, :] = jnp.where(sub == samp // 8, line, 0.0)

    pl.semaphore_wait(barrier, 66)

    def send_tile(step, carry):
        pltpu.make_async_remote_copy(
            src_ref=tiles.at[tile_at],
            dst_ref=tiles.at[tile_at],
            send_sem=tile_send,
            recv_sem=tile_recv,
            device_id={"samp": lax.rem(samp + step, 64), "par": par},
            device_id_type=MESH,
        ).start()
        return carry

    def send_block(piece, x_to, y_to, z_to):
        to = x_to * 32 + y_to * 8 + z_to
        pltpu.make_async_remote_copy(
            src_ref=jac_ref.at[:, pl.ds(pl.multiple_of(to * WIDTH + piece * PIECE, NB), PIECE)],
            dst_ref=held.at[mine, pl.ds(pl.multiple_of(piece * PIECE, NB), PIECE)],
            send_sem=send_sem,
            recv_sem=recv_sem.at[piece],
            device_id={"samp": to, "par": par},
            device_id_type=MESH,
        ).start()

    def send_plane(step, carry):
        piece, plane = step // 8, step % 8
        x_to = (x_hi + 1 - plane // 4) % 2
        y_to = (y + 6 - plane % 4) % 4
        for z_off in (4, 7, 3, 5, 2, 6, 1):
            send_block(piece, x_to, y_to, (z + z_off) % 8)

        @pl.when(plane != 6)
        def _():
            send_block(piece, x_to, y_to, z)

        return carry

    lax.fori_loop(0, 8 * PIECES, send_plane, 0)
    lax.fori_loop(1, 64, send_tile, 0)
    own.wait()

    def work_piece(piece, carry):
        cols = pl.ds(pl.multiple_of(piece * PIECE, NB), PIECE)
        others = held.at[pl.ds(0, N - PER), cols]
        pltpu.make_async_copy(others, others, recv_sem.at[piece]).wait()

        def add_rows(i, total):
            return total + held[pl.ds(pl.multiple_of(i * PER, PER), PER), cols].astype(jnp.float32)

        total = lax.fori_loop(0, N // PER, add_rows, jnp.zeros((PER, PIECE), jnp.float32), unroll=4)
        mean = jnp.sum(total, axis=0, keepdims=True) * (1.0 / N)

        def centre_rows(i, carry):
            at = pl.ds(pl.multiple_of(i * PER, PER), PER)
            held[at, cols] = (held[at, cols].astype(jnp.float32) - mean).astype(jnp.bfloat16)
            return carry

        lax.fori_loop(0, N // PER, centre_rows, 0, unroll=4)
        for i in range(0, BLOCKS, 2):
            size = (i + 2) * NB
            product = lax.dot_general(
                held[i * NB:size, cols], held[0:size, cols], (((1,), (1,)), ((), ())),
                preferred_element_type=jnp.float32,
            )
            for r in range(2):
                for j in range(i + r + 1):
                    at = block_at(i + r, j)
                    packed[at, :] = packed[at, :] + product[r * NB:(r + 1) * NB, j * NB:(j + 1) * NB]
        return carry

    lax.fori_loop(0, PIECES, work_piece, 0)

    slots = (slot_core, slot_one, slot_two, slot_last, staged)
    first_half, second_half, finish = sum_blocks((x, y, z, core), device, packed, final, slots, sum_send, sum_recv)
    first_half()

    others = tiles.at[pl.ds(0, 63 * GR)]
    pltpu.make_async_copy(others, others, tile_recv).wait()
    energy = tiles[0:GR, :]
    for i in range(1, 64):
        energy = energy + tiles[i * GR:(i + 1) * GR, :]

    direction = solve(energy, second_half, final, held, work, x_row, x_col)
    out_ref[...] = direction

    others = held.at[pl.ds(0, N - PER)]
    pltpu.make_async_copy(others, others, send_sem).wait()
    others = tiles.at[pl.ds(0, 63 * GR)]
    pltpu.make_async_copy(others, others, tile_send).wait()
    finish()


def update_call(spin_bits, flip_energy, jacobian):
    anywhere = pl.BlockSpec(memory_space=pl.ANY)
    return pl.pallas_call(
        update_kernel,
        out_shape=jax.ShapeDtypeStruct((1, WIDTH), jnp.float32),
        in_specs=[anywhere, anywhere, anywhere],
        out_specs=pl.BlockSpec(memory_space=pltpu.VMEM),
        scratch_shapes=[
            pltpu.VMEM((PER, SITES), jnp.int32),
            pltpu.VMEM((1, PER), jnp.float32),
            pltpu.VMEM((N, WIDTH), jnp.bfloat16),
            pltpu.VMEM((PACKED, NB), jnp.float32),
            pltpu.VMEM((PACKED, NB), jnp.float32),
            pltpu.VMEM((64 * GR, NB), jnp.float32),
            pltpu.VMEM((2, ROWS_CORE, NB), jnp.float32),
            pltpu.VMEM((2, 4, ROWS_ONE, NB), jnp.float32),
            pltpu.VMEM((2, 4, ROWS_TWO, NB), jnp.float32),
            pltpu.VMEM((2, 8, 2 * ROWS_LAST, NB), jnp.float32),
            pltpu.VMEM((2, 8, 2 * ROWS_LAST, NB), jnp.float32),
            pltpu.VMEM((N + GR, N), jnp.float32),
            pltpu.VMEM((GR, N), jnp.float32),
            pltpu.VMEM((N, NB), jnp.float32),
            pltpu.SemaphoreType.DMA,
            pltpu.SemaphoreType.DMA((PIECES,)),
            pltpu.SemaphoreType.DMA,
            pltpu.SemaphoreType.DMA,
            pltpu.SemaphoreType.DMA,
            pltpu.SemaphoreType.DMA,
            pltpu.SemaphoreType.DMA,
            pltpu.SemaphoreType.DMA((2 * STEPS,)),
            pltpu.SemaphoreType.DMA((2 * STEPS,)),
        ],
        compiler_params=pltpu.CompilerParams(
            collective_id=0, has_side_effects=True, vmem_limit_bytes=60 * 1024 * 1024
        ),
        name="update",
    )(spin_bits, flip_energy.reshape(1, PER), jacobian)


def on_device(spin_bits, flip_energy, jacobian):
    return update_call(spin_bits, flip_energy, jacobian).reshape(1, 1, -1)


def solution(mesh):
    return jax.shard_map(
        on_device,
        mesh=mesh,
        in_specs=(P("samp", None), P("samp"), P("samp", "par")),
        out_specs=P("par", "samp", None),
        check_vma=False,
    )
```

```python
import math

import jax
import jax.numpy as jnp
from jax import lax
from jax.experimental import pallas as pl
from jax.experimental.pallas import tpu as pltpu
from jax.sharding import PartitionSpec as P

SITES = 100
N = 1024
NB = 128
GR = 8
BLOCKS = N // NB
PARAMS = 786432
PER = 16
WIDTH = 3072
PIECES = 6
PIECE = WIDTH // PIECES
PACKED = BLOCKS * (BLOCKS + 1) // 2 * NB
HALF = PACKED // 2
ROWS_CORE = HALF // 2
ROWS_ONE = ROWS_CORE // 4
ROWS_TWO = ROWS_ONE // 4
ROWS_LAST = 8
STEPS = 8
MESH = pl.DeviceIdType.MESH


def block_at(i, j):
    start = (j * BLOCKS - j * (j - 1) // 2 + i - j) * NB
    return slice(start, start + NB)


def bond_weights():
    side = math.isqrt(SITES)
    site = lax.broadcasted_iota(jnp.int32, (SITES, SITES), 0)
    other = lax.broadcasted_iota(jnp.int32, (SITES, SITES), 1)
    row = (site * 205) >> 11
    col = site - row * side

    def bond(down, right):
        to_row, to_col = row + down, col + right
        to_row = jnp.where(to_row >= side, to_row - side, to_row)
        to_col = jnp.where(to_col >= side, to_col - side, jnp.where(to_col < 0, to_col + side, to_col))
        return jnp.where(other == to_row * side + to_col, 1.0, 0.0)

    return 0.25 * (bond(0, 1) + bond(1, 0)) + 0.125 * (bond(1, 1) + bond(1, -1))


def sum_blocks(place, device, packed, final, slots, sum_send, sum_recv):
    x, y, z, core = place
    slot_core, slot_one, slot_two, slot_last, staged = slots
    pos_one = x + core * (y - x)
    pos_two = y + core * (x - y)
    other_core = device(x, y, z, 1 - core)

    def on_one(at):
        return device(at + core * (x - at), y + core * (at - y), z, core)

    def on_two(at):
        return device(x + core * (at - x), at + core * (y - at), z, core)

    def rows(start, size):
        return pl.ds(pl.multiple_of(start, GR), size)

    def send(part, step, source, target, to):
        at = part * STEPS + step
        pltpu.make_async_remote_copy(
            src_ref=source, dst_ref=target, send_sem=sum_send.at[at], recv_sem=sum_recv.at[at],
            device_id=to, device_id_type=MESH,
        ).start()

    def likes(part):
        return (
            slot_core.at[part],
            slot_one.at[part, pl.ds(0, 3)],
            slot_two.at[part, pl.ds(0, 3)],
            slot_last.at[part, pl.ds(0, 7)],
            final.at[pl.ds(0, 7 * ROWS_LAST)],
            final.at[pl.ds(0, 3 * ROWS_TWO)],
            final.at[pl.ds(0, 3 * ROWS_ONE)],
            final.at[pl.ds(0, ROWS_CORE)],
        )

    def arrived(part, step):
        like = likes(part)[step]
        pltpu.make_async_copy(like, like, sum_recv.at[part * STEPS + step]).wait()

    def starts(part):
        half = part * HALF + core * ROWS_CORE
        one = half + pos_one * ROWS_ONE
        return half, one, one + pos_two * ROWS_TWO

    def to_core(part):
        source = packed.at[rows(part * HALF + (1 - core) * ROWS_CORE, ROWS_CORE)]
        send(part, 0, source, slot_core.at[part], other_core)

    def to_one(part):
        half, one, two = starts(part)
        arrived(part, 0)
        packed[rows(half, ROWS_CORE), :] = packed[rows(half, ROWS_CORE), :] + slot_core[part]
        for step in (2, 1, 3):
            to = (pos_one + step) % 4
            send(part, 1, packed.at[rows(half + to * ROWS_ONE, ROWS_ONE)], slot_one.at[part, pos_one], on_one(to))

    def add_three(start, size, slot, part, pos):
        at = rows(start, size)
        packed[at, :] = (packed[at, :] + slot[part, (pos + 1) % 4]) + (
            slot[part, (pos + 2) % 4] + slot[part, (pos + 3) % 4]
        )

    def to_two(part):
        half, one, two = starts(part)
        arrived(part, 1)
        add_three(one, ROWS_ONE, slot_one, part, pos_one)
        for step in (2, 1, 3):
            to = (pos_two + step) % 4
            send(part, 2, packed.at[rows(one + to * ROWS_TWO, ROWS_TWO)], slot_two.at[part, pos_two], on_two(to))

    def to_last(part):
        half, one, two = starts(part)
        arrived(part, 2)
        add_three(two, ROWS_TWO, slot_two, part, pos_two)
        spare = packed[rows(two + 8 * ROWS_LAST, ROWS_LAST), :]
        for i in range(8):
            staged[part, i, 0:ROWS_LAST] = packed[rows(two + i * ROWS_LAST, ROWS_LAST), :]
            staged[part, i, ROWS_LAST:2 * ROWS_LAST] = spare
        for step in (4, 3, 5, 2, 6, 1, 7):
            to = (z + step) % 8
            send(part, 3, staged.at[part, to], slot_last.at[part, z], device(x, y, to, core))

    def back_last(part):
        half, one, two = starts(part)
        slot_last[part, z] = staged[part, z]
        arrived(part, 3)
        total = slot_last[part, 0]
        for i in range(1, 8):
            total = total + slot_last[part, i]
        last = rows(two + z * ROWS_LAST, ROWS_LAST)
        final[last, :] = total[0:ROWS_LAST]
        final[rows(two + 8 * ROWS_LAST, ROWS_LAST), :] = total[ROWS_LAST:2 * ROWS_LAST]
        for step in (4, 3, 5, 2, 6, 1, 7):
            send(part, 4, final.at[last], final.at[last], device(x, y, (z + step) % 8, core))

    def back_two(part):
        half, one, two = starts(part)
        arrived(part, 4)
        for step in (2, 1, 3):
            own = final.at[rows(two, ROWS_TWO)]
            send(part, 5, own, own, on_two((pos_two + step) % 4))

    def back_one(part):
        half, one, two = starts(part)
        arrived(part, 5)
        for step in (2, 1, 3):
            own = final.at[rows(one, ROWS_ONE)]
            send(part, 6, own, own, on_one((pos_one + step) % 4))

    def back_core(part):
        half, one, two = starts(part)
        arrived(part, 6)
        own = final.at[rows(half, ROWS_CORE)]
        send(part, 7, own, own, other_core)

    moves = (to_core, to_one, to_two, to_last, back_last, back_two, back_one, back_core)

    def first_half(between):
        for move in moves:
            for part in range(2):
                move(part)
            if move is to_last:
                result = between()
        arrived(0, STEPS - 1)
        return result

    def second_half():
        arrived(1, STEPS - 1)

    def finish():
        for part in range(2):
            for step in range(STEPS):
                like = likes(part)[step]
                pltpu.make_async_copy(like, like, sum_send.at[part * STEPS + step]).wait()

    return first_half, second_half, finish


def split3(x):
    high = x.astype(jnp.bfloat16)
    rest = x - high.astype(jnp.float32)
    mid = rest.astype(jnp.bfloat16)
    low = (rest - mid.astype(jnp.float32)).astype(jnp.bfloat16)
    return high, mid, low


def dot_wide(a, b, turned=False):
    ah, am, al = split3(a)
    bh, bm, bl = split3(b)
    left = jnp.concatenate([ah, ah, am, am, ah, al], axis=1)
    right = jnp.concatenate([bh, bm, bh, bm, bl, bh], axis=1 if turned else 0)
    dims = (((1,), (1 if turned else 0,)), ((), ()))
    return lax.dot_general(left, right, dims, preferred_element_type=jnp.float32)


def lanes(v, c):
    return jnp.broadcast_to(v[:, c:c + 1], (GR, NB))


def subs(v, r):
    return jnp.broadcast_to(v[r:r + 1, :], (GR, NB))


def add_all(terms):
    while len(terms) > 1:
        terms = [terms[i] + terms[i + 1] for i in range(0, len(terms), 2)]
    return terms[0]


def invert_block(rows):
    lane = lax.broadcasted_iota(jnp.int32, (GR, NB), 1)
    sub = lax.broadcasted_iota(jnp.int32, (GR, NB), 0)
    count = NB // GR
    width = count // 2
    for low in range(0, count, width):
        high = low + width
        piv = [lanes(rows[low], low * GR + c) for c in range(GR)]
        for g in range(low, high):
            base = g * GR
            own = rows[g]
            more = g + 1 < high
            ahead = []
            if more:
                ahead = [lanes(own, base + GR + c) for c in range(GR)]
                coef_next = [lanes(rows[g + 1], base + q) for q in range(GR)]
                piv_next = [lanes(rows[g + 1], base + GR + c) for c in range(GR)]
            in_piv = (lane >= base) & (lane < base + GR)
            row = jnp.where(in_piv, jnp.where(lane - base == sub, 1.0, 0.0), own)
            for q in range(GR):
                at = sub == q
                inv = 1.0 / subs(piv[q], q)
                signed = jnp.where(at, -1.0, piv[q])
                coef = signed * inv
                if q + 1 < GR:
                    piv[q + 1] = jnp.where(at, 0.0, piv[q + 1]) - (signed * subs(piv[q + 1], q)) * inv
                for c in range(q + 2, GR):
                    piv[c] = jnp.where(at, 0.0, piv[c]) - coef * subs(piv[c], q)
                row = jnp.where(at, 0.0, row) - coef * subs(row, q)
                ahead = [jnp.where(at, 0.0, a) - coef * subs(a, q) for a in ahead]
            spread = [subs(row, q) for q in range(GR)]
            if more:
                piv = [
                    piv_next[c] - add_all([coef_next[q] * subs(ahead[c], q) for q in range(GR)]) for c in range(GR)
                ]
            new_rows = list(rows)
            new_rows[g] = row
            for v in [*range(g + 1, high), *range(low, g)]:
                coefs = coef_next if more and v == g + 1 else [lanes(rows[v], base + q) for q in range(GR)]
                new_rows[v] = jnp.where(in_piv, 0.0, rows[v]) - add_all([coefs[q] * spread[q] for q in range(GR)])
            rows = new_rows
        whole = jnp.concatenate(rows, axis=0)
        rest = jnp.concatenate(rows[:low] + rows[high:], axis=0)
        wide_lane = lax.broadcasted_iota(jnp.int32, rest.shape, 1)
        inside = (wide_lane >= low * GR) & (wide_lane < high * GR)
        rest = jnp.where(inside, 0.0, rest) - dot_wide(jnp.where(inside, rest, 0.0), whole)
        parts = [rest[i * GR:(i + 1) * GR, :] for i in range(count - width)]
        rows = parts[:low] + rows[low:high] + parts[low:]
    return rows


def solve(energy, second_half, final, held, work, x_row, x_col):
    sub = lax.broadcasted_iota(jnp.int32, (NB, NB), 0)
    lane = lax.broadcasted_iota(jnp.int32, (NB, NB), 1)
    eye = jnp.where(sub == lane, 1.0, 0.0)

    def unpack(part):
        blocks = [(i, j) for j in range(BLOCKS) for i in range(j, BLOCKS)]
        for i, j in blocks[part * len(blocks) // 2:(part + 1) * len(blocks) // 2]:
            block = final[block_at(i, j), :]
            work[i * NB:(i + 1) * NB, j * NB:(j + 1) * NB] = block + 0.5 * eye if i == j else block

    unpack(0)
    tile = energy
    mean = jnp.sum(jnp.sum(tile, axis=1, keepdims=True), axis=0, keepdims=True) * (1.0 / N)
    tile = tile - mean
    for i in range(BLOCKS):
        work[N:N + GR, i * NB:(i + 1) * NB] = subs(tile, i)

    def stage(k, carry):
        at = pl.ds(pl.multiple_of(k * NB, NB), NB)
        rows = [work[pl.ds(pl.multiple_of(k * NB + v * GR, GR), GR), at] for v in range(NB // GR)]
        rows = invert_block(rows)
        for v in range(NB // GR):
            work[pl.ds(pl.multiple_of(k * NB + v * GR, GR), GR), at] = rows[v]

        @pl.when(k == 0)
        def _():
            second_half()
            unpack(1)

        for c in range(BLOCKS - 1):
            @pl.when(k == c)
            def _():
                own = slice(c * NB, (c + 1) * NB)
                after = slice((c + 1) * NB, N)
                below = slice((c + 1) * NB, N + GR)
                turned = dot_wide(work[own, own], work[after, own], turned=True)
                work[below, after] = work[below, after] - dot_wide(work[below, own], turned)
                work[own, after] = turned
        return carry

    lax.fori_loop(0, BLOCKS, stage, 0)

    direction = jnp.zeros((PER, WIDTH), jnp.float32)
    for k in range(BLOCKS - 1, -1, -1):
        own = slice(k * NB, (k + 1) * NB)
        total = work[own, own] * work[N:N + 1, own]
        for j in range(k + 1, BLOCKS):
            col = slice(j * NB, (j + 1) * NB)
            total = total - work[own, col] * x_row[0:1, col]
        column = jnp.sum(total, axis=1, keepdims=True)
        column = jnp.broadcast_to(column, (NB, NB))
        x_row[0:1, own] = jnp.sum(column * eye, axis=0, keepdims=True)
        x_col[own, :] = column.astype(jnp.bfloat16).astype(jnp.float32)
        if k % 2 == 0:
            pair = slice(k * NB, (k + 2) * NB)
            weights = jnp.broadcast_to(x_row[0:1, pair], (PER, 2 * NB)).astype(jnp.bfloat16)
            direction = direction + jnp.dot(weights, held[pair, :], preferred_element_type=jnp.float32)

    wide = x_row[0:1, :].astype(jnp.bfloat16).astype(jnp.float32)

    acc = jnp.zeros((NB, NB), jnp.float32)
    for i in range(BLOCKS):
        part = final[block_at(i, i), :] * (0.5 * wide[:, i * NB:(i + 1) * NB])
        for j in range(i):
            part = part + final[block_at(i, j), :] * wide[:, j * NB:(j + 1) * NB]
        acc = acc + part * x_col[i * NB:(i + 1) * NB, :]
    square_sum = 2.0 * jnp.sum(jnp.sum(acc, axis=0, keepdims=True), axis=1, keepdims=True)
    root_mean = jnp.sqrt(jnp.maximum(square_sum, 0.0) / PARAMS + 1e-06)
    return -direction[0:1, :] / root_mean


def update_kernel(
    spin_any, flip_any, jac_ref, out_ref,
    spin_ref, flip_ref, held, packed, final, tiles, slot_core, slot_one, slot_two, slot_last, staged, work, x_row, x_col,
    send_sem, recv_sem, own_sem, spin_sem, flip_sem, tile_send, tile_recv, sum_send, sum_recv,
):
    samp, par = lax.axis_index("samp"), lax.axis_index("par")
    core = par % 2
    x_hi, y, z = samp // 32, (samp // 8) % 4, samp % 8
    x = x_hi * 2 + par // 2

    def device(x_at, y_at, z_at, core_at):
        return {"samp": (x_at // 2) * 32 + y_at * 8 + z_at, "par": (x_at % 2) * 2 + core_at}

    spins = pltpu.make_async_copy(spin_any, spin_ref, spin_sem)
    spins.start()
    flips = pltpu.make_async_copy(flip_any, flip_ref, flip_sem)
    flips.start()
    barrier = pltpu.get_barrier_semaphore()

    def greet(step, carry):
        pl.semaphore_signal(
            barrier, inc=1, device_id={"samp": lax.rem(samp + step, 64), "par": par}, device_id_type=MESH
        )
        return carry

    lax.fori_loop(1, 64, greet, 0)
    for partner in (device(x, y, z, 1 - core), device((x + 1) % 4, y, z, core), device((x + 3) % 4, y, z, core)):
        pl.semaphore_signal(barrier, inc=1, device_id=partner, device_id_type=MESH)

    mine = pl.ds(pl.multiple_of(samp * PER, PER), PER)
    own = pltpu.make_async_copy(
        jac_ref.at[:, pl.ds(pl.multiple_of(samp * WIDTH, NB), WIDTH)], held.at[mine], own_sem
    )
    own.start()
    packed[...] = jnp.zeros_like(packed)
    spins.wait()
    flips.wait()

    signs = (2 * spin_ref[...] - 1).astype(jnp.float32).astype(jnp.bfloat16)
    linked = jnp.dot(signs, bond_weights().astype(jnp.bfloat16), preferred_element_type=jnp.float32)
    bonds = jnp.sum(linked * signs.astype(jnp.float32), axis=1, keepdims=True)
    square = (PER, PER)
    same = lax.broadcasted_iota(jnp.int32, square, 0) == lax.broadcasted_iota(jnp.int32, square, 1)
    values = bonds + jnp.sum(jnp.where(same, flip_ref[...], 0.0), axis=1, keepdims=True)
    lane = lax.broadcasted_iota(jnp.int32, (PER, NB), 1)
    sample = lax.broadcasted_iota(jnp.int32, (PER, NB), 0)
    line = jnp.sum(jnp.where(lane == sample + (samp % 8) * PER, values, 0.0), axis=0, keepdims=True)
    sub = lax.broadcasted_iota(jnp.int32, (GR, NB), 0)
    tile_at = pl.ds(pl.multiple_of(samp * GR, GR), GR)
    tiles[tile_at, :] = jnp.where(sub == samp // 8, line, 0.0)

    pl.semaphore_wait(barrier, 66)

    def send_tile(step, carry):
        pltpu.make_async_remote_copy(
            src_ref=tiles.at[tile_at],
            dst_ref=tiles.at[tile_at],
            send_sem=tile_send,
            recv_sem=tile_recv,
            device_id={"samp": lax.rem(samp + step, 64), "par": par},
            device_id_type=MESH,
        ).start()
        return carry

    def send_block(piece, x_to, y_to, z_to):
        to = x_to * 32 + y_to * 8 + z_to
        pltpu.make_async_remote_copy(
            src_ref=jac_ref.at[:, pl.ds(pl.multiple_of(to * WIDTH + piece * PIECE, NB), PIECE)],
            dst_ref=held.at[mine, pl.ds(pl.multiple_of(piece * PIECE, NB), PIECE)],
            send_sem=send_sem,
            recv_sem=recv_sem.at[piece],
            device_id={"samp": to, "par": par},
            device_id_type=MESH,
        ).start()

    def send_plane(step, carry):
        piece, plane = step // 8, step % 8
        x_to = (x_hi + 1 - plane // 4) % 2
        y_to = (y + 6 - plane % 4) % 4
        for z_off in (4, 7, 3, 5, 2, 6, 1):
            send_block(piece, x_to, y_to, (z + z_off) % 8)

        @pl.when(plane != 6)
        def _():
            send_block(piece, x_to, y_to, z)

        return carry

    lax.fori_loop(0, 8 * PIECES, send_plane, 0)
    lax.fori_loop(1, 64, send_tile, 0)
    own.wait()

    def work_piece(piece, carry):
        cols = pl.ds(pl.multiple_of(piece * PIECE, NB), PIECE)
        others = held.at[pl.ds(0, N - PER), cols]
        pltpu.make_async_copy(others, others, recv_sem.at[piece]).wait()

        def add_rows(i, total):
            return total + held[pl.ds(pl.multiple_of(i * PER, PER), PER), cols].astype(jnp.float32)

        total = lax.fori_loop(0, N // PER, add_rows, jnp.zeros((PER, PIECE), jnp.float32), unroll=4)
        mean = jnp.sum(total, axis=0, keepdims=True) * (1.0 / N)

        def centre_rows(i, carry):
            at = pl.ds(pl.multiple_of(i * PER, PER), PER)
            held[at, cols] = (held[at, cols].astype(jnp.float32) - mean).astype(jnp.bfloat16)
            return carry

        lax.fori_loop(0, N // PER, centre_rows, 0, unroll=4)
        for i in range(0, BLOCKS, 2):
            size = (i + 2) * NB
            product = lax.dot_general(
                held[i * NB:size, cols], held[0:size, cols], (((1,), (1,)), ((), ())),
                preferred_element_type=jnp.float32,
            )
            for r in range(2):
                for j in range(i + r + 1):
                    at = block_at(i + r, j)
                    packed[at, :] = packed[at, :] + product[r * NB:(r + 1) * NB, j * NB:(j + 1) * NB]
        return carry

    lax.fori_loop(0, PIECES, work_piece, 0)

    slots = (slot_core, slot_one, slot_two, slot_last, staged)
    first_half, second_half, finish = sum_blocks((x, y, z, core), device, packed, final, slots, sum_send, sum_recv)

    def between():
        others = held.at[pl.ds(0, N - PER)]
        pltpu.make_async_copy(others, others, send_sem).wait()
        others = tiles.at[pl.ds(0, 63 * GR)]
        pltpu.make_async_copy(others, others, tile_send).wait()
        pltpu.make_async_copy(others, others, tile_recv).wait()
        energy = tiles[0:GR, :]
        for i in range(1, 64):
            energy = energy + tiles[i * GR:(i + 1) * GR, :]
        return energy

    energy = first_half(between)
    direction = solve(energy, second_half, final, held, work, x_row, x_col)
    out_ref[...] = direction

    finish()


def update_call(spin_bits, flip_energy, jacobian):
    anywhere = pl.BlockSpec(memory_space=pl.ANY)
    return pl.pallas_call(
        update_kernel,
        out_shape=jax.ShapeDtypeStruct((1, WIDTH), jnp.float32),
        in_specs=[anywhere, anywhere, anywhere],
        out_specs=pl.BlockSpec(memory_space=pltpu.VMEM),
        scratch_shapes=[
            pltpu.VMEM((PER, SITES), jnp.int32),
            pltpu.VMEM((1, PER), jnp.float32),
            pltpu.VMEM((N, WIDTH), jnp.bfloat16),
            pltpu.VMEM((PACKED, NB), jnp.float32),
            pltpu.VMEM((PACKED, NB), jnp.float32),
            pltpu.VMEM((64 * GR, NB), jnp.float32),
            pltpu.VMEM((2, ROWS_CORE, NB), jnp.float32),
            pltpu.VMEM((2, 4, ROWS_ONE, NB), jnp.float32),
            pltpu.VMEM((2, 4, ROWS_TWO, NB), jnp.float32),
            pltpu.VMEM((2, 8, 2 * ROWS_LAST, NB), jnp.float32),
            pltpu.VMEM((2, 8, 2 * ROWS_LAST, NB), jnp.float32),
            pltpu.VMEM((N + GR, N), jnp.float32),
            pltpu.VMEM((GR, N), jnp.float32),
            pltpu.VMEM((N, NB), jnp.float32),
            pltpu.SemaphoreType.DMA,
            pltpu.SemaphoreType.DMA((PIECES,)),
            pltpu.SemaphoreType.DMA,
            pltpu.SemaphoreType.DMA,
            pltpu.SemaphoreType.DMA,
            pltpu.SemaphoreType.DMA,
            pltpu.SemaphoreType.DMA,
            pltpu.SemaphoreType.DMA((2 * STEPS,)),
            pltpu.SemaphoreType.DMA((2 * STEPS,)),
        ],
        compiler_params=pltpu.CompilerParams(
            collective_id=0, has_side_effects=True, vmem_limit_bytes=60 * 1024 * 1024
        ),
        name="update",
    )(spin_bits, flip_energy.reshape(1, PER), jacobian)


def on_device(spin_bits, flip_energy, jacobian):
    return update_call(spin_bits, flip_energy, jacobian).reshape(1, 1, -1)


def solution(mesh):
    return jax.shard_map(
        on_device,
        mesh=mesh,
        in_specs=(P("samp", None), P("samp"), P("samp", "par")),
        out_specs=P("par", "samp", None),
        check_vma=False,
    )
```

```python
import math

import jax
import jax.numpy as jnp
from jax import lax
from jax.experimental import pallas as pl
from jax.experimental.pallas import tpu as pltpu
from jax.sharding import PartitionSpec as P

SITES = 100
N = 1024
NB = 128
GR = 8
BLOCKS = N // NB
PARAMS = 786432
PER = 16
WIDTH = 3072
PIECES = 6
PIECE = WIDTH // PIECES
PACKED = BLOCKS * (BLOCKS + 1) // 2 * NB
HALF = PACKED // 2
ROWS_CORE = HALF // 2
ROWS_ONE = ROWS_CORE // 4
ROWS_TWO = ROWS_ONE // 4
ROWS_LAST = 8
STEPS = 8
MESH = pl.DeviceIdType.MESH


def block_at(i, j):
    start = (j * BLOCKS - j * (j - 1) // 2 + i - j) * NB
    return slice(start, start + NB)


def bond_weights():
    side = math.isqrt(SITES)
    site = lax.broadcasted_iota(jnp.int32, (SITES, SITES), 0)
    other = lax.broadcasted_iota(jnp.int32, (SITES, SITES), 1)
    row = (site * 205) >> 11
    col = site - row * side

    def bond(down, right):
        to_row, to_col = row + down, col + right
        to_row = jnp.where(to_row >= side, to_row - side, to_row)
        to_col = jnp.where(to_col >= side, to_col - side, jnp.where(to_col < 0, to_col + side, to_col))
        return jnp.where(other == to_row * side + to_col, 1.0, 0.0)

    return 0.25 * (bond(0, 1) + bond(1, 0)) + 0.125 * (bond(1, 1) + bond(1, -1))


def sum_blocks(place, device, packed, final, slots, sum_send, sum_recv):
    x, y, z, core = place
    slot_core, slot_one, slot_two, slot_last, staged = slots
    pos_one = x + core * (y - x)
    pos_two = y + core * (x - y)
    other_core = device(x, y, z, 1 - core)

    def on_one(at):
        return device(at + core * (x - at), y + core * (at - y), z, core)

    def on_two(at):
        return device(x + core * (at - x), at + core * (y - at), z, core)

    def rows(start, size):
        return pl.ds(pl.multiple_of(start, GR), size)

    def send(part, step, source, target, to):
        at = part * STEPS + step
        pltpu.make_async_remote_copy(
            src_ref=source, dst_ref=target, send_sem=sum_send.at[at], recv_sem=sum_recv.at[at],
            device_id=to, device_id_type=MESH,
        ).start()

    def likes(part):
        return (
            slot_core.at[part],
            slot_one.at[part, pl.ds(0, 3)],
            slot_two.at[part, pl.ds(0, 3)],
            slot_last.at[part, pl.ds(0, 7)],
            final.at[pl.ds(0, 7 * ROWS_LAST)],
            final.at[pl.ds(0, 3 * ROWS_TWO)],
            final.at[pl.ds(0, 3 * ROWS_ONE)],
            final.at[pl.ds(0, ROWS_CORE)],
        )

    def arrived(part, step):
        like = likes(part)[step]
        pltpu.make_async_copy(like, like, sum_recv.at[part * STEPS + step]).wait()

    def left(part, step):
        like = likes(part)[step]
        pltpu.make_async_copy(like, like, sum_send.at[part * STEPS + step]).wait()

    def starts(part):
        half = part * HALF + core * ROWS_CORE
        one = half + pos_one * ROWS_ONE
        return half, one, one + pos_two * ROWS_TWO

    def to_core(part):
        source = packed.at[rows(part * HALF + (1 - core) * ROWS_CORE, ROWS_CORE)]
        send(part, 0, source, slot_core.at[part], other_core)

    def to_one(part):
        half, one, two = starts(part)
        arrived(part, 0)
        packed[rows(half, ROWS_CORE), :] = packed[rows(half, ROWS_CORE), :] + slot_core[part]
        for step in (2, 1, 3):
            to = (pos_one + step) % 4
            send(part, 1, packed.at[rows(half + to * ROWS_ONE, ROWS_ONE)], slot_one.at[part, pos_one], on_one(to))

    def add_three(start, size, slot, part, pos):
        at = rows(start, size)
        packed[at, :] = (packed[at, :] + slot[part, (pos + 1) % 4]) + (
            slot[part, (pos + 2) % 4] + slot[part, (pos + 3) % 4]
        )

    def to_two(part):
        half, one, two = starts(part)
        arrived(part, 1)
        add_three(one, ROWS_ONE, slot_one, part, pos_one)
        for step in (2, 1, 3):
            to = (pos_two + step) % 4
            send(part, 2, packed.at[rows(one + to * ROWS_TWO, ROWS_TWO)], slot_two.at[part, pos_two], on_two(to))

    def to_last(part):
        half, one, two = starts(part)
        arrived(part, 2)
        add_three(two, ROWS_TWO, slot_two, part, pos_two)
        spare = packed[rows(two + 8 * ROWS_LAST, ROWS_LAST), :]
        for i in range(8):
            staged[part, i, 0:ROWS_LAST] = packed[rows(two + i * ROWS_LAST, ROWS_LAST), :]
            staged[part, i, ROWS_LAST:2 * ROWS_LAST] = spare
        for step in (4, 3, 5, 2, 6, 1, 7):
            to = (z + step) % 8
            send(part, 3, staged.at[part, to], slot_last.at[part, z], device(x, y, to, core))

    def back_last(part):
        half, one, two = starts(part)
        slot_last[part, z] = staged[part, z]
        arrived(part, 3)
        total = slot_last[part, 0]
        for i in range(1, 8):
            total = total + slot_last[part, i]
        last = rows(two + z * ROWS_LAST, ROWS_LAST)
        final[last, :] = total[0:ROWS_LAST]
        final[rows(two + 8 * ROWS_LAST, ROWS_LAST), :] = total[ROWS_LAST:2 * ROWS_LAST]
        for step in (4, 3, 5, 2, 6, 1, 7):
            send(part, 4, final.at[last], final.at[last], device(x, y, (z + step) % 8, core))

    def back_two(part):
        half, one, two = starts(part)
        arrived(part, 4)
        for step in (2, 1, 3):
            own = final.at[rows(two, ROWS_TWO)]
            send(part, 5, own, own, on_two((pos_two + step) % 4))

    def back_one(part):
        half, one, two = starts(part)
        arrived(part, 5)
        for step in (2, 1, 3):
            own = final.at[rows(one, ROWS_ONE)]
            send(part, 6, own, own, on_one((pos_one + step) % 4))

    def back_core(part):
        half, one, two = starts(part)
        arrived(part, 6)
        own = final.at[rows(half, ROWS_CORE)]
        send(part, 7, own, own, other_core)

    moves = (to_core, to_one, to_two, to_last, back_last, back_two, back_one, back_core)

    def first_half(between):
        for move in moves:
            for part in range(2):
                move(part)
            if move is to_last:
                result = between()
        for part in range(2):
            for step in range(STEPS - 1):
                left(part, step)
        arrived(0, STEPS - 1)
        return result

    def second_half():
        arrived(1, STEPS - 1)

    def finish():
        for part in range(2):
            left(part, STEPS - 1)

    return first_half, second_half, finish


def split3(x):
    high = x.astype(jnp.bfloat16)
    rest = x - high.astype(jnp.float32)
    mid = rest.astype(jnp.bfloat16)
    low = (rest - mid.astype(jnp.float32)).astype(jnp.bfloat16)
    return high, mid, low


def dot_wide(a, b, turned=False):
    ah, am, al = split3(a)
    bh, bm, bl = split3(b)
    left = jnp.concatenate([ah, ah, am, am, ah, al], axis=1)
    right = jnp.concatenate([bh, bm, bh, bm, bl, bh], axis=1 if turned else 0)
    dims = (((1,), (1 if turned else 0,)), ((), ()))
    return lax.dot_general(left, right, dims, preferred_element_type=jnp.float32)


def lanes(v, c):
    return jnp.broadcast_to(v[:, c:c + 1], (GR, NB))


def subs(v, r):
    return jnp.broadcast_to(v[r:r + 1, :], (GR, NB))


def add_all(terms):
    while len(terms) > 1:
        terms = [terms[i] + terms[i + 1] for i in range(0, len(terms), 2)]
    return terms[0]


def invert_block(rows):
    lane = lax.broadcasted_iota(jnp.int32, (GR, NB), 1)
    sub = lax.broadcasted_iota(jnp.int32, (GR, NB), 0)
    count = NB // GR
    width = count // 2
    for low in range(0, count, width):
        high = low + width
        piv = [lanes(rows[low], low * GR + c) for c in range(GR)]
        for g in range(low, high):
            base = g * GR
            own = rows[g]
            more = g + 1 < high
            ahead = []
            if more:
                ahead = [lanes(own, base + GR + c) for c in range(GR)]
                coef_next = [lanes(rows[g + 1], base + q) for q in range(GR)]
                piv_next = [lanes(rows[g + 1], base + GR + c) for c in range(GR)]
            in_piv = (lane >= base) & (lane < base + GR)
            row = jnp.where(in_piv, jnp.where(lane - base == sub, 1.0, 0.0), own)
            for q in range(GR):
                at = sub == q
                inv = 1.0 / subs(piv[q], q)
                signed = jnp.where(at, -1.0, piv[q])
                coef = signed * inv
                if q + 1 < GR:
                    piv[q + 1] = jnp.where(at, 0.0, piv[q + 1]) - (signed * subs(piv[q + 1], q)) * inv
                for c in range(q + 2, GR):
                    piv[c] = jnp.where(at, 0.0, piv[c]) - coef * subs(piv[c], q)
                row = jnp.where(at, 0.0, row) - coef * subs(row, q)
                ahead = [jnp.where(at, 0.0, a) - coef * subs(a, q) for a in ahead]
            spread = [subs(row, q) for q in range(GR)]
            if more:
                piv = [
                    piv_next[c] - add_all([coef_next[q] * subs(ahead[c], q) for q in range(GR)]) for c in range(GR)
                ]
            new_rows = list(rows)
            new_rows[g] = row
            for v in [*range(g + 1, high), *range(low, g)]:
                coefs = coef_next if more and v == g + 1 else [lanes(rows[v], base + q) for q in range(GR)]
                new_rows[v] = jnp.where(in_piv, 0.0, rows[v]) - add_all([coefs[q] * spread[q] for q in range(GR)])
            rows = new_rows
        whole = jnp.concatenate(rows, axis=0)
        rest = jnp.concatenate(rows[:low] + rows[high:], axis=0)
        wide_lane = lax.broadcasted_iota(jnp.int32, rest.shape, 1)
        inside = (wide_lane >= low * GR) & (wide_lane < high * GR)
        rest = jnp.where(inside, 0.0, rest) - dot_wide(jnp.where(inside, rest, 0.0), whole)
        parts = [rest[i * GR:(i + 1) * GR, :] for i in range(count - width)]
        rows = parts[:low] + rows[low:high] + parts[low:]
    return rows


def solve(energy, second_half, final, held, work, x_row, x_col):
    sub = lax.broadcasted_iota(jnp.int32, (NB, NB), 0)
    lane = lax.broadcasted_iota(jnp.int32, (NB, NB), 1)
    eye = jnp.where(sub == lane, 1.0, 0.0)

    def unpack(part):
        blocks = [(i, j) for j in range(BLOCKS) for i in range(j, BLOCKS)]
        for i, j in blocks[part * len(blocks) // 2:(part + 1) * len(blocks) // 2]:
            block = final[block_at(i, j), :]
            work[i * NB:(i + 1) * NB, j * NB:(j + 1) * NB] = block + 0.5 * eye if i == j else block

    unpack(0)
    tile = energy
    mean = jnp.sum(jnp.sum(tile, axis=1, keepdims=True), axis=0, keepdims=True) * (1.0 / N)
    tile = tile - mean
    for i in range(BLOCKS):
        work[N:N + GR, i * NB:(i + 1) * NB] = subs(tile, i)

    def stage(k, carry):
        at = pl.ds(pl.multiple_of(k * NB, NB), NB)
        rows = [work[pl.ds(pl.multiple_of(k * NB + v * GR, GR), GR), at] for v in range(NB // GR)]
        rows = invert_block(rows)
        for v in range(NB // GR):
            work[pl.ds(pl.multiple_of(k * NB + v * GR, GR), GR), at] = rows[v]

        @pl.when(k == 0)
        def _():
            second_half()
            unpack(1)

        for c in range(BLOCKS - 1):
            @pl.when(k == c)
            def _():
                own = slice(c * NB, (c + 1) * NB)
                after = slice((c + 1) * NB, N)
                below = slice((c + 1) * NB, N + GR)
                turned = dot_wide(work[own, own], work[after, own], turned=True)
                work[below, after] = work[below, after] - dot_wide(work[below, own], turned)
                work[own, after] = turned
        return carry

    lax.fori_loop(0, BLOCKS, stage, 0)

    direction = jnp.zeros((PER, WIDTH), jnp.float32)
    for k in range(BLOCKS - 1, -1, -1):
        own = slice(k * NB, (k + 1) * NB)
        total = work[own, own] * work[N:N + 1, own]
        for j in range(k + 1, BLOCKS):
            col = slice(j * NB, (j + 1) * NB)
            total = total - work[own, col] * x_row[0:1, col]
        column = jnp.sum(total, axis=1, keepdims=True)
        column = jnp.broadcast_to(column, (NB, NB))
        x_row[0:1, own] = jnp.sum(column * eye, axis=0, keepdims=True)
        x_col[own, :] = column.astype(jnp.bfloat16).astype(jnp.float32)
        if k % 2 == 0:
            pair = slice(k * NB, (k + 2) * NB)
            weights = jnp.broadcast_to(x_row[0:1, pair], (PER, 2 * NB)).astype(jnp.bfloat16)
            direction = direction + jnp.dot(weights, held[pair, :], preferred_element_type=jnp.float32)

    wide = x_row[0:1, :].astype(jnp.bfloat16).astype(jnp.float32)

    acc = jnp.zeros((NB, NB), jnp.float32)
    for i in range(BLOCKS):
        part = final[block_at(i, i), :] * (0.5 * wide[:, i * NB:(i + 1) * NB])
        for j in range(i):
            part = part + final[block_at(i, j), :] * wide[:, j * NB:(j + 1) * NB]
        acc = acc + part * x_col[i * NB:(i + 1) * NB, :]
    square_sum = 2.0 * jnp.sum(jnp.sum(acc, axis=0, keepdims=True), axis=1, keepdims=True)
    root_mean = jnp.sqrt(jnp.maximum(square_sum, 0.0) / PARAMS + 1e-06)
    return -direction[0:1, :] / root_mean


def update_kernel(
    spin_any, flip_any, jac_ref, out_ref,
    spin_ref, flip_ref, held, packed, final, tiles, slot_core, slot_one, slot_two, slot_last, staged, work, x_row, x_col,
    send_sem, recv_sem, own_sem, spin_sem, flip_sem, tile_send, tile_recv, sum_send, sum_recv,
):
    samp, par = lax.axis_index("samp"), lax.axis_index("par")
    core = par % 2
    x_hi, y, z = samp // 32, (samp // 8) % 4, samp % 8
    x = x_hi * 2 + par // 2

    def device(x_at, y_at, z_at, core_at):
        return {"samp": (x_at // 2) * 32 + y_at * 8 + z_at, "par": (x_at % 2) * 2 + core_at}

    spins = pltpu.make_async_copy(spin_any, spin_ref, spin_sem)
    spins.start()
    flips = pltpu.make_async_copy(flip_any, flip_ref, flip_sem)
    flips.start()
    barrier = pltpu.get_barrier_semaphore()

    def greet(step, carry):
        pl.semaphore_signal(
            barrier, inc=1, device_id={"samp": lax.rem(samp + 1 + lax.rem(step + 30, 63), 64), "par": par}, device_id_type=MESH
        )
        return carry

    lax.fori_loop(1, 64, greet, 0)
    for partner in (device(x, y, z, 1 - core), device((x + 1) % 4, y, z, core), device((x + 3) % 4, y, z, core)):
        pl.semaphore_signal(barrier, inc=1, device_id=partner, device_id_type=MESH)

    mine = pl.ds(pl.multiple_of(samp * PER, PER), PER)
    own = pltpu.make_async_copy(
        jac_ref.at[:, pl.ds(pl.multiple_of(samp * WIDTH, NB), WIDTH)], held.at[mine], own_sem
    )
    own.start()
    packed[...] = jnp.zeros_like(packed)
    spins.wait()
    flips.wait()

    signs = (2 * spin_ref[...] - 1).astype(jnp.float32).astype(jnp.bfloat16)
    linked = jnp.dot(signs, bond_weights().astype(jnp.bfloat16), preferred_element_type=jnp.float32)
    bonds = jnp.sum(linked * signs.astype(jnp.float32), axis=1, keepdims=True)
    square = (PER, PER)
    same = lax.broadcasted_iota(jnp.int32, square, 0) == lax.broadcasted_iota(jnp.int32, square, 1)
    values = bonds + jnp.sum(jnp.where(same, flip_ref[...], 0.0), axis=1, keepdims=True)
    lane = lax.broadcasted_iota(jnp.int32, (PER, NB), 1)
    sample = lax.broadcasted_iota(jnp.int32, (PER, NB), 0)
    line = jnp.sum(jnp.where(lane == sample + (samp % 8) * PER, values, 0.0), axis=0, keepdims=True)
    sub = lax.broadcasted_iota(jnp.int32, (GR, NB), 0)
    tile_at = pl.ds(pl.multiple_of(samp * GR, GR), GR)
    tiles[tile_at, :] = jnp.where(sub == samp // 8, line, 0.0)

    pl.semaphore_wait(barrier, 66)

    def send_tile(step, carry):
        pltpu.make_async_remote_copy(
            src_ref=tiles.at[tile_at],
            dst_ref=tiles.at[tile_at],
            send_sem=tile_send,
            recv_sem=tile_recv,
            device_id={"samp": lax.rem(samp + step, 64), "par": par},
            device_id_type=MESH,
        ).start()
        return carry

    def send_block(piece, x_to, y_to, z_to):
        to = x_to * 32 + y_to * 8 + z_to
        pltpu.make_async_remote_copy(
            src_ref=jac_ref.at[:, pl.ds(pl.multiple_of(to * WIDTH + piece * PIECE, NB), PIECE)],
            dst_ref=held.at[mine, pl.ds(pl.multiple_of(piece * PIECE, NB), PIECE)],
            send_sem=send_sem,
            recv_sem=recv_sem.at[piece],
            device_id={"samp": to, "par": par},
            device_id_type=MESH,
        ).start()

    def send_plane(step, carry):
        piece, plane = step // 8, step % 8
        x_to = (x_hi + 1 - plane // 4) % 2
        y_to = (y + 6 - plane % 4) % 4
        for z_off in (4, 7, 3, 5, 2, 6, 1):
            send_block(piece, x_to, y_to, (z + z_off) % 8)

        @pl.when(plane != 6)
        def _():
            send_block(piece, x_to, y_to, z)

        return carry

    lax.fori_loop(0, 8 * PIECES, send_plane, 0)
    lax.fori_loop(1, 64, send_tile, 0)
    own.wait()

    def work_piece(piece, carry):
        cols = pl.ds(pl.multiple_of(piece * PIECE, NB), PIECE)
        others = held.at[pl.ds(0, N - PER), cols]
        pltpu.make_async_copy(others, others, recv_sem.at[piece]).wait()

        def add_rows(i, total):
            return total + held[pl.ds(pl.multiple_of(i * PER, PER), PER), cols].astype(jnp.float32)

        total = lax.fori_loop(0, N // PER, add_rows, jnp.zeros((PER, PIECE), jnp.float32), unroll=4)
        mean = jnp.sum(total, axis=0, keepdims=True) * (1.0 / N)

        def centre_rows(i, carry):
            at = pl.ds(pl.multiple_of(i * PER, PER), PER)
            held[at, cols] = (held[at, cols].astype(jnp.float32) - mean).astype(jnp.bfloat16)
            return carry

        lax.fori_loop(0, N // PER, centre_rows, 0, unroll=4)
        for i in range(0, BLOCKS, 2):
            size = (i + 2) * NB
            product = lax.dot_general(
                held[i * NB:size, cols], held[0:size, cols], (((1,), (1,)), ((), ())),
                preferred_element_type=jnp.float32,
            )
            for r in range(2):
                for j in range(i + r + 1):
                    at = block_at(i + r, j)
                    packed[at, :] = packed[at, :] + product[r * NB:(r + 1) * NB, j * NB:(j + 1) * NB]
        return carry

    lax.fori_loop(0, PIECES, work_piece, 0)

    slots = (slot_core, slot_one, slot_two, slot_last, staged)
    first_half, second_half, finish = sum_blocks((x, y, z, core), device, packed, final, slots, sum_send, sum_recv)

    def between():
        others = held.at[pl.ds(0, N - PER)]
        pltpu.make_async_copy(others, others, send_sem).wait()
        others = tiles.at[pl.ds(0, 63 * GR)]
        pltpu.make_async_copy(others, others, tile_send).wait()
        pltpu.make_async_copy(others, others, tile_recv).wait()
        energy = tiles[0:GR, :]
        for i in range(1, 64):
            energy = energy + tiles[i * GR:(i + 1) * GR, :]
        return energy

    energy = first_half(between)
    direction = solve(energy, second_half, final, held, work, x_row, x_col)
    out_ref[...] = direction

    finish()


def update_call(spin_bits, flip_energy, jacobian):
    anywhere = pl.BlockSpec(memory_space=pl.ANY)
    return pl.pallas_call(
        update_kernel,
        out_shape=jax.ShapeDtypeStruct((1, WIDTH), jnp.float32),
        in_specs=[anywhere, anywhere, anywhere],
        out_specs=pl.BlockSpec(memory_space=pltpu.VMEM),
        scratch_shapes=[
            pltpu.VMEM((PER, SITES), jnp.int32),
            pltpu.VMEM((1, PER), jnp.float32),
            pltpu.VMEM((N, WIDTH), jnp.bfloat16),
            pltpu.VMEM((PACKED, NB), jnp.float32),
            pltpu.VMEM((PACKED, NB), jnp.float32),
            pltpu.VMEM((64 * GR, NB), jnp.float32),
            pltpu.VMEM((2, ROWS_CORE, NB), jnp.float32),
            pltpu.VMEM((2, 4, ROWS_ONE, NB), jnp.float32),
            pltpu.VMEM((2, 4, ROWS_TWO, NB), jnp.float32),
            pltpu.VMEM((2, 8, 2 * ROWS_LAST, NB), jnp.float32),
            pltpu.VMEM((2, 8, 2 * ROWS_LAST, NB), jnp.float32),
            pltpu.VMEM((N + GR, N), jnp.float32),
            pltpu.VMEM((GR, N), jnp.float32),
            pltpu.VMEM((N, NB), jnp.float32),
            pltpu.SemaphoreType.DMA,
            pltpu.SemaphoreType.DMA((PIECES,)),
            pltpu.SemaphoreType.DMA,
            pltpu.SemaphoreType.DMA,
            pltpu.SemaphoreType.DMA,
            pltpu.SemaphoreType.DMA,
            pltpu.SemaphoreType.DMA,
            pltpu.SemaphoreType.DMA((2 * STEPS,)),
            pltpu.SemaphoreType.DMA((2 * STEPS,)),
        ],
        compiler_params=pltpu.CompilerParams(
            collective_id=0, has_side_effects=True, vmem_limit_bytes=60 * 1024 * 1024
        ),
        name="update",
    )(spin_bits, flip_energy.reshape(1, PER), jacobian)


def on_device(spin_bits, flip_energy, jacobian):
    return update_call(spin_bits, flip_energy, jacobian).reshape(1, 1, -1)


def solution(mesh):
    return jax.shard_map(
        on_device,
        mesh=mesh,
        in_specs=(P("samp", None), P("samp"), P("samp", "par")),
        out_specs=P("par", "samp", None),
        check_vma=False,
    )
```
